768 devices in a mesh: row: 64 (over x, y, core), col: 12 (over z).
Axes of the slice: x: 4, y: 8, z: 12, core: 2. Of those that a mesh axis runs over, the one named last changes fastest.
Arguments:
- object_field: float32 [2, 2, 16384, 3072], P(None, None, 'row', 'col'), may hold values from -4 to 4
- probe: float32 [2, 2, 256, 256], replicated, may hold values from -3 to 3
- scan_positions: int32 [64, 12, 1, 2], P('row', 'col'), may hold values from 0 to 16128, as said below
- amplitudes: float32 [64, 12, 1, 256, 256], P('row', 'col'), may hold values from 0.2 to 1.8
Outputs:
- object_gradient: float32 [2, 2, 16384, 3072], P(None, None, 'row', 'col')
- probe_gradient: float32 [2, 2, 256, 256], replicated
The draws below stay inside these ranges and needn't reach their ends.
Inputs may be any that keep to these rules, and one draw needn't show every extreme that they name: scan_positions[i, j, n] holds the row and the column of the upper left pixel of a 256 x 256 patch; the row lies in [i * 256, i * 256 + 256), the column in [j * 256, j * 256 + 256), and every patch lies inside the object; position 0 of device (0, 0) is at (0, 0) and position 0 of the last device is at (16128, 2816).
All inputs are finite; a program needn't handle non-finite values.
Results may differ from the reference program's by a relative error of at most 0.0003.
Values sent between devices are 32-bit elements; how exact they have to be, the bound alone decides.
A program may use at most 32 MiB of HBM per device.

```python
import math
import jax
import jax.numpy as jnp
from jax import lax

P_SIZE = 256
MODES = 2
L = 2
TR = 256
TC = 256
POS_DEV = 1
ROWS = 16384
COLS = 3072
POSITIONS = 768
N_ROW = 64
N_COL = 12


def draw_scan_positions(key, part):
    tiles_down = ROWS // TR
    tiles_across = COLS // TC
    key_rows, key_cols = jax.random.split(jax.random.fold_in(key, 17))
    shape_grid = (tiles_down, tiles_across, POS_DEV)
    down_steps = jax.random.randint(key_rows, shape_grid, 0, TR)
    across_steps = jax.random.randint(key_cols, shape_grid, 0, TC)
    row_tiles = jnp.arange(tiles_down, dtype=jnp.int32)[:, None, None]
    col_tiles = jnp.arange(tiles_across, dtype=jnp.int32)[None, :, None]
    slot_index = jnp.arange(POS_DEV, dtype=jnp.int32)[None, None, :]
    down_span = jnp.where(row_tiles == tiles_down - 1, TR - P_SIZE + 1, TR)
    across_span = jnp.where(col_tiles == tiles_across - 1, TC - P_SIZE + 1, TC)
    rows_at = row_tiles * TR + down_steps % down_span
    cols_at = col_tiles * TC + across_steps % across_span
    first_slot = (row_tiles == 0) & (col_tiles == 0) & (slot_index == 0)
    last_slot = (row_tiles == tiles_down - 1) & (col_tiles == tiles_across - 1) & (slot_index == 0)
    rows_at = jnp.where(first_slot, 0, jnp.where(last_slot, ROWS - P_SIZE, rows_at))
    cols_at = jnp.where(first_slot, 0, jnp.where(last_slot, COLS - P_SIZE, cols_at))
    return jnp.stack([rows_at, cols_at], axis=-1).astype(jnp.int32)


def block_scale(stream_key, extent, cuts, low, top_value):
    def one(position, blocks):
        heights = jax.random.uniform(jax.random.fold_in(jax.random.fold_in(stream_key, 6), position), (blocks,), jnp.float32, low / len(cuts), top_value / len(cuts))
        return jnp.repeat(jnp.exp(heights), extent[position] // blocks).reshape((-1,) + (1,) * (len(extent) - position - 1))

    factor_of = one(*cuts[0])
    for cut in cuts[1:]:
        factor_of = factor_of * one(*cut)
    return factor_of


def noise(own_key, dims, scale, bound, cuts=(), held_as=jnp.bfloat16):
    level = block_scale(own_key, dims, cuts, -0.22, 0.18) if cuts else 1.0
    result = jax.random.normal(own_key, dims, jnp.float32) * scale * level
    return jnp.minimum(jnp.maximum(result, -bound), bound).astype(held_as)


def setup_inputs(seed: int = 0) -> dict:
    streams_of = jax.random.split(jax.random.key(seed), 5)
    return {
        "object_field": noise(streams_of[0], (L, 2, ROWS, COLS), 0.7, 4.0, ((2, 64), (3, 12)), jnp.float32),
        "probe": noise(streams_of[1], (MODES, 2, P_SIZE, P_SIZE), 0.5, 3.0, (), jnp.float32),
        "scan_positions": draw_scan_positions(jax.random.fold_in(streams_of[4], 71), 0),
        "amplitudes": jnp.clip(0.2 + 1.5999999 * jax.random.uniform(streams_of[3], (N_ROW, N_COL, POS_DEV, P_SIZE, P_SIZE), jnp.float32) ** block_scale(streams_of[3], (N_ROW, N_COL, POS_DEV, P_SIZE, P_SIZE), ((0, 64), (1, 12)), -0.2, 0.2), 0.2, 1.8),
    }


intensity_floor = 0.5
chirp_divisor = 2.0

def complex_blocks(matrix_real, matrix_imag):
    left_block = jnp.stack([jnp.stack([matrix_real, -matrix_imag], axis=1), jnp.stack([matrix_imag, matrix_real], axis=1)], axis=0)
    real_t = matrix_real.T
    imag_t = matrix_imag.T
    right_block = jnp.stack([jnp.stack([real_t, imag_t], axis=1), jnp.stack([-imag_t, real_t], axis=1)], axis=0)
    return (left_block, right_block)

def tables(order_dft):
    indices = jnp.arange(order_dft, dtype=jnp.int32)
    products = indices[:, None] * indices[None, :] % order_dft
    angles = 2.0 * math.pi / order_dft * products.astype(jnp.float32)
    norm_factor = 1.0 / math.sqrt(order_dft)
    dft_real = jnp.cos(angles) * norm_factor
    dft_imag = -jnp.sin(angles) * norm_factor
    centered = jnp.where(indices < order_dft // 2, indices, indices - order_dft).astype(jnp.float32)
    chirp_phase = -math.pi * centered * centered / (chirp_divisor * order_dft)
    phase_real = jnp.cos(chirp_phase)
    phase_imag = jnp.sin(chirp_phase)
    shifted_real = phase_real[:, None] * dft_real - phase_imag[:, None] * dft_imag
    shifted_imag = phase_real[:, None] * dft_imag + phase_imag[:, None] * dft_real
    highest = lax.Precision.HIGHEST
    kernel_real = jnp.dot(dft_real, shifted_real, precision=highest) + jnp.dot(dft_imag, shifted_imag, precision=highest)
    kernel_imag = jnp.dot(dft_real, shifted_imag, precision=highest) - jnp.dot(dft_imag, shifted_real, precision=highest)
    dft_left, dft_right = complex_blocks(dft_real, dft_imag)
    kernel_left, kernel_right = complex_blocks(kernel_real, kernel_imag)
    return (dft_left, dft_right, kernel_left, kernel_right)

def apply_both(left_block, right_block, field):
    highest = lax.Precision.HIGHEST
    field = jnp.einsum('satb,mtbc->msac', left_block, field, precision=highest)
    return jnp.einsum('mtab,tbsc->msac', field, right_block, precision=highest)

def complex_times(field, factor):
    out_real = field[:, 0] * factor[0] - field[:, 1] * factor[1]
    out_imag = field[:, 0] * factor[1] + field[:, 1] * factor[0]
    return jnp.stack([out_real, out_imag], axis=1)

def position_loss(probe, object_patch, amplitude_block, tables_dft):
    dft_left, dft_right, kernel_left, kernel_right = tables_dft
    wave = complex_times(probe, object_patch[0])
    for slice_number in range(1, object_patch.shape[0]):
        wave = apply_both(kernel_left, kernel_right, wave)
        wave = complex_times(wave, object_patch[slice_number])
    far = apply_both(dft_left, dft_right, wave)
    intensity = lax.optimization_barrier(jnp.sum(far * far, axis=(0, 1)))
    return jnp.sum((jnp.sqrt(intensity + intensity_floor) - amplitude_block) ** 2)

def position_grads(probe, object_patch, amplitude_block, tables_dft):
    misfit, pullback = jax.vjp(lambda probe_in, patch_in: position_loss(probe_in, patch_in, amplitude_block, tables_dft), probe, object_patch)
    return pullback(jnp.ones_like(misfit))

def reference(object_field, probe, scan_positions, amplitudes):
    tables_dft = tables(P_SIZE)
    flat_positions = scan_positions.reshape(-1, 2)
    flat_amplitudes = amplitudes.reshape(-1, P_SIZE, P_SIZE)

    def advance(state, entry):
        object_grads, probe_grads = state
        corner, amplitude_block = entry
        anchor = jnp.zeros((), jnp.int32)
        corner_start = (anchor, anchor, corner[0].astype(jnp.int32), corner[1].astype(jnp.int32))
        object_patch = lax.dynamic_slice(object_field, corner_start, (L, 2, P_SIZE, P_SIZE))
        probe_part, patch_part = position_grads(probe, object_patch, amplitude_block, tables_dft)
        previous = lax.dynamic_slice(object_grads, corner_start, (L, 2, P_SIZE, P_SIZE))
        object_grads = lax.dynamic_update_slice(object_grads, previous + patch_part, corner_start)
        return ((object_grads, probe_grads + probe_part), None)
    start_state = (jnp.zeros(object_field.shape, jnp.float32), jnp.zeros(probe.shape, jnp.float32))
    (object_grads, probe_grads), _ = lax.scan(advance, start_state, (flat_positions, flat_amplitudes))
    return (object_grads, probe_grads / math.sqrt(POSITIONS))
```

```python
import math

import jax
import jax.numpy as jnp
from jax import lax
from jax.experimental import pallas as pl
from jax.experimental.pallas import tpu as pltpu
from jax.sharding import PartitionSpec as P

intensity_floor = 0.5
chirp_divisor = 2.0
MESH_ID = pl.DeviceIdType.MESH


def place():
    row = lax.axis_index("row")
    return row // 16, (row // 2) % 8, lax.axis_index("col"), row % 2


def device(x, y, z, core):
    return ((x * 8 + y) * 2 + core, z)


def start_copy(source, target, sent, landed, to):
    copy = pltpu.make_async_remote_copy(
        src_ref=source, dst_ref=target, send_sem=sent, recv_sem=landed, device_id=to, device_id_type=MESH_ID
    )
    copy.start()


def wait_bytes(ref, semaphore):
    pltpu.make_async_copy(ref, ref, semaphore).wait()


class ProbeSum:
    def __init__(self, parts, total, from_core, near, from_x, mid, from_y, from_z, sent, landed, scale):
        self.parts, self.total, self.from_core, self.near = parts, total, from_core, near
        self.from_x, self.mid, self.from_y, self.from_z = from_x, mid, from_y, from_z
        self.sent, self.landed, self.scale = sent, landed, scale
        self.x, self.y, self.z, self.core = place()

    def x_peers(self):
        return [lax.rem(self.x + d, 4) for d in range(1, 4)]

    def y_peers(self):
        return [lax.rem(self.y + d, 8) for d in range(1, 8)]

    def z_peers(self):
        return [lax.rem(self.z + d, 12) for d in range(1, 12)]

    def columns(self, chunk):
        return chunk // 2, pl.ds(128 * (chunk % 2), 128)

    def stage(self, chunk, step):
        x, y, z, core = self.x, self.y, self.z, self.core
        mode, lanes = self.columns(chunk)
        other = device(x, y, z, 1 - core)
        sent, landed = self.sent.at[chunk, step], self.landed.at[chunk, step]
        arrived = self.landed.at[chunk, step - 1]
        mine = pl.ds(pl.multiple_of(64 * x + 8 * y, 8), 8)
        block = pl.ds(pl.multiple_of(64 * x, 64), 64)
        if step == 0:
            start_copy(self.parts.at[mode, 1 - core, :, lanes], self.from_core.at[chunk], sent, landed, other)
        elif step == 1:
            wait_bytes(self.from_core.at[chunk], arrived)
            self.near[chunk] = self.parts[mode, core, :, lanes] + self.from_core[chunk]
            for d, px in enumerate(self.x_peers()):
                rows = pl.ds(pl.multiple_of(64 * px, 64), 64)
                start_copy(self.near.at[chunk, rows], self.from_x.at[chunk, d], sent, landed, device(px, y, z, core))
        elif step == 2:
            wait_bytes(self.from_x.at[chunk], arrived)
            self.mid[chunk] = (self.near[chunk, block, :] + self.from_x[chunk, 0]) + (
                self.from_x[chunk, 1] + self.from_x[chunk, 2]
            )
            for d, py in enumerate(self.y_peers()):
                rows = pl.ds(pl.multiple_of(8 * py, 8), 8)
                start_copy(self.mid.at[chunk, rows], self.from_y.at[chunk, d], sent, landed, device(x, py, z, core))
        elif step == 3:
            wait_bytes(self.from_y.at[chunk], arrived)
            piece = self.mid[chunk, pl.ds(pl.multiple_of(8 * y, 8), 8), :]
            for d in range(7):
                piece = piece + self.from_y[chunk, d]
            self.from_z[chunk, z] = piece
            for pz in self.z_peers():
                start_copy(self.from_z.at[chunk, z], self.from_z.at[chunk, z], sent, landed, device(x, y, pz, core))
        elif step == 4:
            wait_bytes(self.from_z.at[chunk, pl.ds(0, 11)], arrived)
            piece = self.from_z[chunk, 0]
            for d in range(1, 12):
                piece = piece + self.from_z[chunk, d]
            self.total[mode, core, mine, lanes] = piece * self.scale
            spot = self.total.at[mode, core, mine, lanes]
            for py in self.y_peers():
                start_copy(spot, spot, sent, landed, device(x, py, z, core))
        elif step == 5:
            wait_bytes(self.total.at[mode, core, pl.ds(0, 56), lanes], arrived)
            spot = self.total.at[mode, core, block, lanes]
            for px in self.x_peers():
                start_copy(spot, spot, sent, landed, device(px, y, z, core))
        elif step == 6:
            wait_bytes(self.total.at[mode, core, pl.ds(0, 192), lanes], arrived)
            spot = self.total.at[mode, core, :, lanes]
            start_copy(spot, spot, sent, landed, other)
        elif step == 7:
            wait_bytes(self.total.at[mode, core, :, lanes], arrived)

    def drain(self, chunk):
        mode, lanes = self.columns(chunk)
        sizes = [
            self.from_core.at[chunk],
            self.from_x.at[chunk],
            self.from_y.at[chunk],
            self.from_z.at[chunk, pl.ds(0, 11)],
            self.total.at[mode, self.core, pl.ds(0, 56), lanes],
            self.total.at[mode, self.core, pl.ds(0, 192), lanes],
            self.total.at[mode, self.core, :, lanes],
        ]
        for step, ref in enumerate(sizes):
            wait_bytes(ref, self.sent.at[chunk, step])

    def greet(self, barrier):
        x, y, z, core = self.x, self.y, self.z, self.core
        peers = [device(x, y, z, 1 - core)]
        peers += [device(px, y, z, core) for px in self.x_peers()]
        peers += [device(x, py, z, core) for py in self.y_peers()]
        peers += [device(x, y, pz, core) for pz in self.z_peers()]
        for peer in peers:
            pl.semaphore_signal(barrier, inc=1, device_id=peer, device_id_type=MESH_ID)
        return len(peers)


PROBE_SUM_SCRATCH = [
    pltpu.VMEM((4, 256, 128), jnp.float32),
    pltpu.VMEM((4, 256, 128), jnp.float32),
    pltpu.VMEM((4, 3, 64, 128), jnp.float32),
    pltpu.VMEM((4, 64, 128), jnp.float32),
    pltpu.VMEM((4, 7, 8, 128), jnp.float32),
    pltpu.VMEM((4, 12, 8, 128), jnp.float32),
    pltpu.SemaphoreType.DMA((4, 7)),
    pltpu.SemaphoreType.DMA((4, 7)),
]


def probe_sum_kernel(parts, total, *scratch):
    total_sum = ProbeSum(parts, total, *scratch, 1.0 / math.sqrt(768))
    barrier = pltpu.get_barrier_semaphore()
    count = total_sum.greet(barrier)
    pl.semaphore_wait(barrier, count)
    for step in range(8):
        for chunk in range(4):
            total_sum.stage(chunk, step)
    for chunk in range(4):
        total_sum.drain(chunk)


def probe_sum(parts):
    return pl.pallas_call(
        probe_sum_kernel,
        out_shape=jax.ShapeDtypeStruct((2, 2, 256, 256), jnp.float32),
        in_specs=[pl.BlockSpec(memory_space=pltpu.VMEM)],
        out_specs=pl.BlockSpec(memory_space=pltpu.VMEM),
        scratch_shapes=PROBE_SUM_SCRATCH,
        compiler_params=pltpu.CompilerParams(collective_id=0, has_side_effects=True, vmem_limit_bytes=32 << 20),
    )(parts)


def from_behind(array, axis, by):
    count = lax.axis_size(axis)
    pairs = [(i, i + by) for i in range(count) if 0 <= i + by < count]
    return lax.ppermute(array, axis, pairs)


def complex_blocks(matrix_real, matrix_imag):
    left_block = jnp.stack(
        [
            jnp.stack([matrix_real, -matrix_imag], axis=1),
            jnp.stack([matrix_imag, matrix_real], axis=1),
        ],
        axis=0,
    )
    real_t = matrix_real.T
    imag_t = matrix_imag.T
    right_block = jnp.stack(
        [jnp.stack([real_t, imag_t], axis=1), jnp.stack([-imag_t, real_t], axis=1)], axis=0
    )
    return (left_block, right_block)


def tables(order_dft):
    indices = jnp.arange(order_dft, dtype=jnp.int32)
    products = indices[:, None] * indices[None, :] % order_dft
    angles = 2.0 * math.pi / order_dft * products.astype(jnp.float32)
    norm_factor = 1.0 / math.sqrt(order_dft)
    dft_real = jnp.cos(angles) * norm_factor
    dft_imag = -jnp.sin(angles) * norm_factor
    centered = jnp.where(indices < order_dft // 2, indices, indices - order_dft).astype(jnp.float32)
    chirp_phase = -math.pi * centered * centered / (chirp_divisor * order_dft)
    phase_real = jnp.cos(chirp_phase)
    phase_imag = jnp.sin(chirp_phase)
    shifted_real = phase_real[:, None] * dft_real - phase_imag[:, None] * dft_imag
    shifted_imag = phase_real[:, None] * dft_imag + phase_imag[:, None] * dft_real
    highest = lax.Precision.HIGHEST
    kernel_real = jnp.dot(dft_real, shifted_real, precision=highest) + jnp.dot(
        dft_imag, shifted_imag, precision=highest
    )
    kernel_imag = jnp.dot(dft_real, shifted_imag, precision=highest) - jnp.dot(
        dft_imag, shifted_real, precision=highest
    )
    dft_left, dft_right = complex_blocks(dft_real, dft_imag)
    kernel_left, kernel_right = complex_blocks(kernel_real, kernel_imag)
    return (dft_left, dft_right, kernel_left, kernel_right)


def apply_both(left_block, right_block, field):
    highest = lax.Precision.HIGHEST
    field = jnp.einsum("satb,mtbc->msac", left_block, field, precision=highest)
    return jnp.einsum("mtab,tbsc->msac", field, right_block, precision=highest)


def complex_times(field, factor):
    out_real = field[:, 0] * factor[0] - field[:, 1] * factor[1]
    out_imag = field[:, 0] * factor[1] + field[:, 1] * factor[0]
    return jnp.stack([out_real, out_imag], axis=1)


def position_loss(probe, object_patch, amplitude_block, tables_dft):
    dft_left, dft_right, kernel_left, kernel_right = tables_dft
    wave = complex_times(probe, object_patch[0])
    wave = apply_both(kernel_left, kernel_right, wave)
    wave = complex_times(wave, object_patch[1])
    far = apply_both(dft_left, dft_right, wave)
    intensity = jnp.sum(far * far, axis=(0, 1))
    return jnp.sum((jnp.sqrt(intensity + intensity_floor) - amplitude_block) ** 2)


def position_grads(probe, object_patch, amplitude_block, tables_dft):
    misfit, pullback = jax.vjp(
        lambda probe_in, patch_in: position_loss(probe_in, patch_in, amplitude_block, tables_dft),
        probe,
        object_patch,
    )
    return pullback(jnp.ones_like(misfit))


def on_device(object_field, probe, scan_positions, amplitudes):
    layers, halves, tile_rows, tile_cols = object_field.shape
    probe_width = probe.shape[-1]
    tables_dft = tables(probe_width)
    right_rim = from_behind(object_field, "col", -1)
    widened = jnp.concatenate([object_field, right_rim], axis=3)
    below_rim = from_behind(widened, "row", -1)
    extended = jnp.concatenate([widened, below_rim], axis=2)
    row_base = lax.axis_index("row") * tile_rows
    col_base = lax.axis_index("col") * tile_cols
    anchor = jnp.zeros((), jnp.int32)
    object_grads = jnp.zeros(extended.shape, jnp.float32)
    corner = scan_positions[0, 0, 0]
    row_start = corner[0] - row_base
    col_start = corner[1] - col_base
    corner_start = (anchor, anchor, row_start, col_start)
    object_patch = lax.dynamic_slice(
        extended, corner_start, (layers, halves, probe_width, probe_width)
    )
    probe_part, patch_part = position_grads(probe, object_patch, amplitudes[0, 0, 0], tables_dft)
    object_grads = lax.dynamic_update_slice(object_grads, patch_part, corner_start)
    from_above = from_behind(object_grads[:, :, tile_rows:, :], "row", 1)
    upper_rows = object_grads[:, :, :tile_rows, :].at[:, :, :probe_width, :].add(from_above)
    from_left = from_behind(upper_rows[:, :, :, tile_cols:], "col", 1)
    object_gradient = upper_rows[:, :, :, :tile_cols].at[:, :, :, :probe_width].add(from_left)
    probe_gradient = probe_sum(probe_part)
    return (object_gradient, probe_gradient)


def solution(mesh):
    in_specs = (
        P(None, None, "row", "col"),
        P(),
        P("row", "col", None, None),
        P("row", "col", None, None, None),
    )
    out_specs = (P(None, None, "row", "col"), P())
    return jax.shard_map(
        on_device, mesh=mesh, in_specs=in_specs, out_specs=out_specs, check_vma=False
    )
```

```python
import functools
import math

import jax
import jax.numpy as jnp
import ml_dtypes
import numpy as np
from jax import lax
from jax.experimental import pallas as pl
from jax.experimental.pallas import tpu as pltpu
from jax.sharding import PartitionSpec as P

intensity_floor = 0.5
chirp_divisor = 2.0
WIDTH = 256
HALF = 128
ROWS, COLS = 64, 12
VMEM = pl.BlockSpec(memory_space=pltpu.VMEM)
f32, bf16 = jnp.float32, jnp.bfloat16


def right_form(matrix):
    return np.block([[matrix.real, matrix.imag], [-matrix.imag, matrix.real]])


def left_form(matrix):
    return np.block([[matrix.real, -matrix.imag], [matrix.imag, matrix.real]])


def in_two(block):
    high = block.astype(np.float32).astype(ml_dtypes.bfloat16)
    low = (block - high.astype(np.float64)).astype(np.float32).astype(ml_dtypes.bfloat16)
    return high, low


def for_right(block):
    high, low = in_two(block)
    return np.concatenate([high, high, low], axis=0)


def for_left(block):
    high, low = in_two(block)
    return np.concatenate([high, low, high], axis=1)


@functools.lru_cache
def tables():
    indices = np.arange(WIDTH)
    turns = (indices[:, None] * indices[None, :]) % WIDTH
    dft = np.exp(-2j * np.pi * turns / WIDTH) / np.sqrt(WIDTH)
    centered = np.where(indices < HALF, indices, indices - WIDTH).astype(np.float64)
    phase = np.exp(-1j * np.pi * centered**2 / (chirp_divisor * WIDTH))
    kernel = np.conj(dft) @ (phase[:, None] * dft)
    near, far = kernel[:HALF, :HALF], kernel[:HALF, HALF:]
    halves = [(near + far) / 2, (near - far) / 2]
    combs = [dft[:HALF, 0::2], dft[:HALF, 1::2]]
    forms = {
        "kernel_right": [for_right(right_form(m)) for m in halves],
        "kernel_left": [for_left(left_form(m)) for m in halves],
        "kernel_right_back": [for_right(left_form(m)) for m in halves],
        "kernel_left_back": [for_left(right_form(m)) for m in halves],
        "dft_right": [for_right(right_form(m)) for m in combs],
        "dft_left": [for_left(left_form(m.T)) for m in combs],
        "dft_right_back": [for_right(left_form(m.T)) for m in combs],
        "dft_left_back": [for_left(right_form(m)) for m in combs],
    }
    return {name: np.stack(pair) for name, pair in forms.items()}


def split(value):
    high = value.astype(bf16)
    return high, (value - high.astype(f32)).astype(bf16)


def times_right(field, table):
    high, low = split(field)
    return jnp.dot(jnp.concatenate([high, low, high], axis=1), table, preferred_element_type=f32)


def times_left(table, field):
    high, low = split(field)
    return jnp.dot(table, jnp.concatenate([high, high, low], axis=0), preferred_element_type=f32)


def both_sides(combs, right, left):
    turned = [times_right(combs[e], right[e]) for e in range(2)]
    out = []
    for e in range(2):
        slabs = []
        for mode in range(2):
            start = mode * WIDTH + e * HALF
            rows = [turned[k][start : start + HALF] for k in range(2)]
            top = jnp.concatenate([rows[0][:, :HALF], rows[1][:, :HALF]], axis=1)
            bottom = jnp.concatenate([rows[0][:, HALF:], rows[1][:, HALF:]], axis=1)
            slabs.append(jnp.concatenate([top, bottom], axis=0))
        out.append(times_left(left[e], jnp.concatenate(slabs, axis=1)))
    return out


def butterfly(plane):
    plane = jnp.concatenate([plane[:HALF] + plane[HALF:], plane[:HALF] - plane[HALF:]], axis=0)
    return plane[:, :HALF] + plane[:, HALF:], plane[:, :HALF] - plane[:, HALF:]


def fold(waves):
    parts = [(butterfly(re), butterfly(im)) for re, im in waves]
    return [
        jnp.concatenate([jnp.concatenate([re[e], im[e]], axis=1) for re, im in parts], axis=0) for e in range(2)
    ]


def comb_fields(fields):
    return [
        jnp.concatenate(
            [jnp.concatenate([part[:, e * HALF : (e + 1) * HALF] for part in pair], axis=1) for pair in fields], axis=0
        )
        for e in range(2)
    ]


def plane_of(out, mode, part):
    lanes = slice(mode * WIDTH, (mode + 1) * WIDTH)
    rows = slice(part * HALF, (part + 1) * HALF)
    return [out[e][rows, lanes] for e in range(2)]


def unfold(out):
    def spread(mode, part):
        even, odd = plane_of(out, mode, part)
        plane = jnp.concatenate([even + odd, even - odd], axis=0)
        even, odd = plane[:, :HALF], plane[:, HALF:]
        return jnp.concatenate([even + odd, even - odd], axis=1)

    return [(spread(mode, 0), spread(mode, 1)) for mode in range(2)]


def in_combs(out):
    return [tuple(jnp.concatenate(plane_of(out, mode, part), axis=0) for part in range(2)) for mode in range(2)]


def times(a, b):
    return a[0] * b[0] - a[1] * b[1], a[0] * b[1] + a[1] * b[0]


def times_conj(a, b):
    return a[0] * b[0] + a[1] * b[1], a[1] * b[0] - a[0] * b[1]


def iota(axis):
    return lax.broadcasted_iota(jnp.int32, (WIDTH, WIDTH), axis)


def one_hot(condition):
    return jnp.where(condition, 1.0, 0.0).astype(bf16)


def permute(left, planes, right):
    count = len(planes)
    high, low = split(jnp.concatenate(planes, axis=1))
    moved = jnp.dot(left, high, preferred_element_type=f32) + jnp.dot(left, low, preferred_element_type=f32)
    rows = jnp.concatenate([moved[:, k * WIDTH : (k + 1) * WIDTH] for k in range(count)], axis=0)
    high, low = split(rows)
    moved = jnp.dot(high, right, preferred_element_type=f32) + jnp.dot(low, right, preferred_element_type=f32)
    return [moved[k * WIDTH : (k + 1) * WIDTH] for k in range(count)]


MESH_ID = pl.DeviceIdType.MESH


def place():
    row = lax.axis_index("row")
    return row // 16, (row // 2) % 8, lax.axis_index("col"), row % 2


def device(x, y, z, core):
    return ((x * 8 + y) * 2 + core, z)


def start_copy(source, target, sent, landed, to):
    copy = pltpu.make_async_remote_copy(
        src_ref=source, dst_ref=target, send_sem=sent, recv_sem=landed, device_id=to, device_id_type=MESH_ID
    )
    copy.start()
    return copy


def wait_bytes(ref, semaphore):
    pltpu.make_async_copy(ref, ref, semaphore).wait()


class ProbeSum:
    def __init__(self, parts, total, from_core, near, from_x, mid, from_y, from_z, sent, landed, scale):
        self.parts, self.total, self.from_core, self.near = parts, total, from_core, near
        self.from_x, self.mid, self.from_y, self.from_z = from_x, mid, from_y, from_z
        self.sent, self.landed, self.scale = sent, landed, scale
        self.x, self.y, self.z, self.core = place()

    def x_peers(self):
        return [lax.rem(self.x + d, 4) for d in range(1, 4)]

    def y_peers(self):
        return [lax.rem(self.y + d, 8) for d in range(1, 8)]

    def z_peers(self):
        return [lax.rem(self.z + d, 12) for d in range(1, 12)]

    def columns(self, chunk):
        return chunk // 2, pl.ds(128 * (chunk % 2), 128)

    def stage(self, chunk, step):
        x, y, z, core = self.x, self.y, self.z, self.core
        mode, lanes = self.columns(chunk)
        other = device(x, y, z, 1 - core)
        sent, landed = self.sent.at[chunk, step], self.landed.at[chunk, step]
        arrived = self.landed.at[chunk, step - 1]
        mine = pl.ds(pl.multiple_of(64 * x + 8 * y, 8), 8)
        block = pl.ds(pl.multiple_of(64 * x, 64), 64)
        if step == 0:
            start_copy(self.parts.at[mode, 1 - core, :, lanes], self.from_core.at[chunk], sent, landed, other)
        elif step == 1:
            wait_bytes(self.from_core.at[chunk], arrived)
            self.near[chunk] = self.parts[mode, core, :, lanes] + self.from_core[chunk]
            for d, px in enumerate(self.x_peers()):
                rows = pl.ds(pl.multiple_of(64 * px, 64), 64)
                start_copy(self.near.at[chunk, rows], self.from_x.at[chunk, d], sent, landed, device(px, y, z, core))
        elif step == 2:
            wait_bytes(self.from_x.at[chunk], arrived)
            self.mid[chunk] = (self.near[chunk, block, :] + self.from_x[chunk, 0]) + (
                self.from_x[chunk, 1] + self.from_x[chunk, 2]
            )
            for d, py in enumerate(self.y_peers()):
                rows = pl.ds(pl.multiple_of(8 * py, 8), 8)
                start_copy(self.mid.at[chunk, rows], self.from_y.at[chunk, d], sent, landed, device(x, py, z, core))
        elif step == 3:
            wait_bytes(self.from_y.at[chunk], arrived)
            piece = self.mid[chunk, pl.ds(pl.multiple_of(8 * y, 8), 8), :]
            for d in range(7):
                piece = piece + self.from_y[chunk, d]
            self.from_z[chunk, z] = piece
            for pz in self.z_peers():
                start_copy(self.from_z.at[chunk, z], self.from_z.at[chunk, z], sent, landed, device(x, y, pz, core))
        elif step == 4:
            wait_bytes(self.from_z.at[chunk, pl.ds(0, 11)], arrived)
            piece = self.from_z[chunk, 0]
            for d in range(1, 12):
                piece = piece + self.from_z[chunk, d]
            self.total[mode, core, mine, lanes] = piece * self.scale
            spot = self.total.at[mode, core, mine, lanes]
            for py in self.y_peers():
                start_copy(spot, spot, sent, landed, device(x, py, z, core))
        elif step == 5:
            wait_bytes(self.total.at[mode, core, pl.ds(0, 56), lanes], arrived)
            spot = self.total.at[mode, core, block, lanes]
            for px in self.x_peers():
                start_copy(spot, spot, sent, landed, device(px, y, z, core))
        elif step == 6:
            wait_bytes(self.total.at[mode, core, pl.ds(0, 192), lanes], arrived)
            spot = self.total.at[mode, core, :, lanes]
            start_copy(spot, spot, sent, landed, other)
        elif step == 7:
            wait_bytes(self.total.at[mode, core, :, lanes], arrived)

    def drain(self, chunk):
        mode, lanes = self.columns(chunk)
        sizes = [
            self.from_core.at[chunk],
            self.from_x.at[chunk],
            self.from_y.at[chunk],
            self.from_z.at[chunk, pl.ds(0, 11)],
            self.total.at[mode, self.core, pl.ds(0, 56), lanes],
            self.total.at[mode, self.core, pl.ds(0, 192), lanes],
            self.total.at[mode, self.core, :, lanes],
        ]
        for step, ref in enumerate(sizes):
            wait_bytes(ref, self.sent.at[chunk, step])

    def greet(self, barrier):
        x, y, z, core = self.x, self.y, self.z, self.core
        peers = [device(x, y, z, 1 - core)]
        peers += [device(px, y, z, core) for px in self.x_peers()]
        peers += [device(x, py, z, core) for py in self.y_peers()]
        peers += [device(x, y, pz, core) for pz in self.z_peers()]
        for peer in peers:
            pl.semaphore_signal(barrier, inc=1, device_id=peer, device_id_type=MESH_ID)
        return len(peers)


PROBE_SUM_SCRATCH = [
    pltpu.VMEM((4, 256, 128), jnp.float32),
    pltpu.VMEM((4, 256, 128), jnp.float32),
    pltpu.VMEM((4, 3, 64, 128), jnp.float32),
    pltpu.VMEM((4, 64, 128), jnp.float32),
    pltpu.VMEM((4, 7, 8, 128), jnp.float32),
    pltpu.VMEM((4, 12, 8, 128), jnp.float32),
    pltpu.SemaphoreType.DMA((4, 7)),
    pltpu.SemaphoreType.DMA((4, 7)),
]


def halo_kernel(
    tile, probe, corner, amplitude, kernel_right, kernel_left,
    patch, moved_probe, wave, spectrum, corners,
    below, merged, side, left_corner, own_spectrum, side_spectrum, sent, landed,
):
    row, z = lax.axis_index("row"), lax.axis_index("col")
    core = lax.rem(row, 2)
    up, down = (lax.rem(row + ROWS - 1, ROWS), z), (lax.rem(row + 1, ROWS), z)
    right, left = (row, lax.rem(z + 1, COLS)), (row, lax.rem(z + COLS - 1, COLS))
    onward = (row, lax.rem(z + COLS - 1 + 2 * core, COLS))
    barrier = pltpu.get_barrier_semaphore()
    for peer in (up, down, right, left):
        pl.semaphore_signal(barrier, inc=1, device_id=peer, device_id_type=MESH_ID)

    rows, lanes = iota(0), iota(1)
    to_combs = one_hot(lanes == 2 * lax.rem(rows, HALF) + rows // HALF)
    from_combs = one_hot(rows == 2 * lax.rem(lanes, HALF) + lanes // HALF)
    own_spectrum[...] = permute(to_combs, [amplitude[...]], from_combs)[0]
    pl.semaphore_wait(barrier, 4)

    def chunk(index):
        layer, part, half = index // 4, (index // 2) % 2, index % 2
        return layer, part, pl.ds(half * HALF, HALF)

    copies = [start_copy(corner, left_corner, sent.at[16], landed.at[16], right)]
    for index in range(8):
        spot = chunk(index)
        copies.append(start_copy(tile.at[spot], below.at[spot], sent.at[index], landed.at[index], up))

    @pl.when(core == 1)
    def _():
        start_copy(own_spectrum, side_spectrum, sent.at[17], landed.at[17], right)

    wait_bytes(left_corner, landed.at[16])
    own, other = corner[...], left_corner[...]
    working = own + core * (other - own)
    handing = other + core * (own - other)
    row_start, col_start = working[0:1, :], working[1:2, :]
    hand_start = handing[0:1, :]
    corners[0] = working
    corners[1] = handing

    for index in range(8):
        layer, part, span = chunk(index)
        wait_bytes(below.at[layer, part, span], landed.at[index])
        mine, under = tile[layer, part, span, :], below[layer, part, span, :]
        merged[layer, part, span, :] = jnp.where(rows[span.start : span.start + HALF] >= hand_start, mine, under)
        spot = merged.at[layer, part, span]
        copies.append(start_copy(spot, side.at[layer, part, span], sent.at[8 + index], landed.at[8 + index], onward))
        patch[layer, part, span, :] = jnp.where(rows[span.start : span.start + HALF] >= row_start, mine, under)
        if index == 3:
            shift_rows = one_hot(jnp.bitwise_and(rows - lanes - row_start, WIDTH - 1) == 0)
            shift_cols = one_hot(jnp.bitwise_and(lanes - rows - col_start, WIDTH - 1) == 0)
            planes = [probe[mode, part] for mode in range(2) for part in range(2)]
            for k, plane in enumerate(permute(shift_rows, planes, shift_cols)):
                moved_probe[k // 2, k % 2] = plane

    own_columns = jnp.where(lanes >= col_start, 1, 0) != core

    def finish(layer):
        for index in range(4):
            wait_bytes(side.at[chunk(4 * layer + index)], landed.at[8 + 4 * layer + index])
        for part in range(2):
            patch[layer, part] = jnp.where(own_columns, patch[layer, part], side[layer, part])

    finish(0)
    first = (patch[0, 0], patch[0, 1])
    waves = [times((moved_probe[mode, 0], moved_probe[mode, 1]), first) for mode in range(2)]
    for mode, pair in enumerate(unfold(both_sides(fold(waves), kernel_right, kernel_left))):
        for part in range(2):
            wave[mode, part] = pair[part]
    finish(1)

    @pl.when(core == 0)
    def _():
        spectrum[...] = own_spectrum[...]

    @pl.when(core == 1)
    def _():
        wait_bytes(side_spectrum, landed.at[17])
        spectrum[...] = side_spectrum[...]
        wait_bytes(side_spectrum, sent.at[17])

    for copy in copies:
        copy.wait_send()


def halo_in(tile, probe, corner, amplitude, names):
    shape = lambda *dims: jax.ShapeDtypeStruct(dims, f32)
    full = (2, 2, WIDTH, WIDTH)
    return pl.pallas_call(
        halo_kernel,
        out_shape=[
            shape(*full), shape(*full), shape(*full), shape(WIDTH, WIDTH), jax.ShapeDtypeStruct((2, 8, WIDTH), jnp.int32),
        ],
        in_specs=[VMEM] * 6,
        out_specs=[VMEM] * 5,
        scratch_shapes=[
            pltpu.VMEM(full, f32),
            pltpu.VMEM(full, f32),
            pltpu.VMEM(full, f32),
            pltpu.VMEM((8, WIDTH), jnp.int32),
            pltpu.VMEM((WIDTH, WIDTH), f32),
            pltpu.VMEM((WIDTH, WIDTH), f32),
            pltpu.SemaphoreType.DMA((18,)),
            pltpu.SemaphoreType.DMA((18,)),
        ],
        compiler_params=pltpu.CompilerParams(collective_id=1, has_side_effects=True, vmem_limit_bytes=48 << 20),
    )(tile, probe, corner, amplitude, names["kernel_right"], names["kernel_left"])


def gradient_kernel(
    patch, moved_probe, wave, spectrum, corners,
    dft_right, dft_left, dft_right_back, dft_left_back, kernel_right_back, kernel_left_back,
    object_gradient, total,
    parts, side_out, side_in, down_out, down_in, grads, sent, landed, *scratch,
):
    probe_total = ProbeSum(parts, total, *scratch, 1.0 / math.sqrt(ROWS * COLS))
    row, z = lax.axis_index("row"), lax.axis_index("col")
    core = lax.rem(row, 2)
    up, down = (lax.rem(row + ROWS - 1, ROWS), z), (lax.rem(row + 1, ROWS), z)
    back = (row, lax.rem(z + 1 + (COLS - 2) * core, COLS))
    barrier = pltpu.get_barrier_semaphore()
    count = probe_total.greet(barrier)
    for peer in (up, down):
        pl.semaphore_signal(barrier, inc=1, device_id=peer, device_id_type=MESH_ID)

    rows, lanes = iota(0), iota(1)
    row_start, col_start, hand_start = corners[0, 0:1, :], corners[0, 1:2, :], corners[1, 0:1, :]
    own_columns = jnp.where(lanes >= col_start, 1, 0) != core
    second = (patch[1, 0], patch[1, 1])
    waves = [(wave[mode, 0], wave[mode, 1]) for mode in range(2)]
    passed = [times(pair, second) for pair in waves]
    far = in_combs(both_sides(fold(passed), dft_right, dft_left))
    intensity = far[0][0] * far[0][0] + far[0][1] * far[0][1] + (far[1][0] * far[1][0] + far[1][1] * far[1][1])
    weight = 2.0 - 2.0 * spectrum[...] * lax.rsqrt(intensity + intensity_floor)
    far = [(weight * re, weight * im) for re, im in far]
    slope = unfold(both_sides(comb_fields(far), dft_right_back, dft_left_back))
    pl.semaphore_wait(barrier, count + 2)
    copies = []

    def send_side(layer, terms):
        for part in range(2):
            grads[layer, part] = terms[0][part] + terms[1][part]
            side_out[layer, part] = jnp.where(own_columns, 0.0, grads[layer, part])
        copies.append(start_copy(side_out.at[layer], side_in.at[layer], sent.at[layer], landed.at[layer], back))

    def send_down(layer):
        wait_bytes(side_in.at[layer], landed.at[layer])
        for part in range(2):
            mine = jnp.where(own_columns, grads[layer, part], 0.0)
            other = side_in[layer, part]
            down_out[layer, part] = jnp.where(rows < row_start, mine, 0.0) + jnp.where(rows < hand_start, other, 0.0)
            grads[layer, part] = jnp.where(rows < row_start, 0.0, mine) + jnp.where(rows < hand_start, 0.0, other)
        copies.append(start_copy(down_out.at[layer], down_in.at[layer], sent.at[2 + layer], landed.at[2 + layer], down))

    def finish(layer):
        wait_bytes(down_in.at[layer], landed.at[2 + layer])
        object_gradient[layer] = grads[layer] + down_in[layer]

    send_side(1, [times_conj(slope[mode], waves[mode]) for mode in range(2)])
    slope = [times_conj(pair, second) for pair in slope]
    slope = unfold(both_sides(fold(slope), kernel_right_back, kernel_left_back))
    first = (patch[0, 0], patch[0, 1])
    shift_rows = one_hot(jnp.bitwise_and(lanes - rows - row_start, WIDTH - 1) == 0)
    shift_cols = one_hot(jnp.bitwise_and(rows - lanes - col_start, WIDTH - 1) == 0)
    for mode in range(2):
        for part, plane in enumerate(permute(shift_rows, list(times_conj(slope[mode], first)), shift_cols)):
            parts[mode, part] = plane
        for chunk in range(2):
            probe_total.stage(2 * mode + chunk, 0)
    send_side(0, [times_conj(slope[mode], (moved_probe[mode, 0], moved_probe[mode, 1])) for mode in range(2)])
    for step in range(1, 8):
        for chunk in range(4):
            probe_total.stage(chunk, step)
        if step == 2:
            send_down(1)
        if step == 3:
            send_down(0)
        if step == 5:
            finish(1)
        if step == 6:
            finish(0)
    for chunk in range(4):
        probe_total.drain(chunk)
    for copy in copies:
        copy.wait_send()


def gradients(patch, moved_probe, wave, spectrum, corners, names):
    full = (2, 2, WIDTH, WIDTH)
    return pl.pallas_call(
        gradient_kernel,
        out_shape=[jax.ShapeDtypeStruct(full, f32)] * 2,
        in_specs=[VMEM] * 11,
        out_specs=[VMEM] * 2,
        scratch_shapes=[pltpu.VMEM(full, f32)] * 6
        + [pltpu.SemaphoreType.DMA((4,)), pltpu.SemaphoreType.DMA((4,))]
        + PROBE_SUM_SCRATCH,
        compiler_params=pltpu.CompilerParams(collective_id=2, has_side_effects=True, vmem_limit_bytes=48 << 20),
    )(
        patch, moved_probe, wave, spectrum, corners,
        names["dft_right"], names["dft_left"], names["dft_right_back"], names["dft_left_back"],
        names["kernel_right_back"], names["kernel_left_back"],
    )


def on_device(object_field, probe, scan_positions, amplitudes):
    names = {name: jnp.asarray(table) for name, table in tables().items()}
    tile_rows, tile_cols = object_field.shape[2:]
    base = jnp.stack([lax.axis_index("row") * tile_rows, lax.axis_index("col") * tile_cols])
    corner = scan_positions[0, 0, 0] - base
    corner = jnp.broadcast_to(jnp.pad(corner, (0, 6))[:, None], (8, WIDTH))
    held = halo_in(object_field, probe, corner, amplitudes[0, 0, 0], names)
    return tuple(gradients(*held, names))


def solution(mesh):
    in_specs = (
        P(None, None, "row", "col"),
        P(),
        P("row", "col", None, None),
        P("row", "col", None, None, None),
    )
    out_specs = (P(None, None, "row", "col"), P())
    return jax.shard_map(
        on_device, mesh=mesh, in_specs=in_specs, out_specs=out_specs, check_vma=False
    )
```

```python
import functools
import math

import jax
import jax.numpy as jnp
import ml_dtypes
import numpy as np
from jax import lax
from jax.experimental import pallas as pl
from jax.experimental.pallas import tpu as pltpu
from jax.sharding import PartitionSpec as P

intensity_floor = 0.5
chirp_divisor = 2.0
WIDTH = 256
HALF = 128
ROWS, COLS = 64, 12
f32, bf16 = jnp.float32, jnp.bfloat16


def right_form(matrix):
    return np.block([[matrix.real, matrix.imag], [-matrix.imag, matrix.real]])


def left_form(matrix):
    return np.block([[matrix.real, -matrix.imag], [matrix.imag, matrix.real]])


@functools.lru_cache
def tables():
    indices = np.arange(WIDTH)
    turns = (indices[:, None] * indices[None, :]) % WIDTH
    dft = np.exp(-2j * np.pi * turns / WIDTH) / np.sqrt(WIDTH)
    centered = np.where(indices < HALF, indices, indices - WIDTH).astype(np.float64)
    phase = np.exp(-1j * np.pi * centered**2 / (chirp_divisor * WIDTH))
    kernel = np.conj(dft) @ (phase[:, None] * dft)
    near, far = kernel[:HALF, :HALF], kernel[:HALF, HALF:]
    halves = [(near + far) / 2, (near - far) / 2]
    combs = [dft[:HALF, 0::2], dft[:HALF, 1::2]]
    blocks = np.stack(
        [
            [right_form(m) for m in halves],
            [left_form(m) for m in halves],
            [right_form(m) for m in combs],
            [left_form(m.T) for m in combs],
        ]
    )
    high = blocks.astype(np.float32).astype(ml_dtypes.bfloat16)
    low = (blocks - high.astype(np.float64)).astype(np.float32).astype(ml_dtypes.bfloat16)
    return np.stack([high, low], axis=2)


KERNEL, KERNEL_BACK, DFT, DFT_BACK = (0, 1), (1, 0), (2, 3), (3, 2)


def split(value):
    high = value.astype(bf16)
    return high, (value - high.astype(f32)).astype(bf16)


def times_right(field, table):
    high, low = split(field)
    blocks = jnp.concatenate([table[0], table[0], table[1]], axis=0)
    return jnp.dot(jnp.concatenate([high, low, high], axis=1), blocks, preferred_element_type=f32)


def times_left(table, field):
    high, low = split(field)
    blocks = jnp.concatenate([table[0], table[1], table[0]], axis=1)
    return jnp.dot(blocks, jnp.concatenate([high, high, low], axis=0), preferred_element_type=f32)


def both_sides(combs, table, sides):
    right, left = sides
    turned = [times_right(combs[e], table[right, e]) for e in range(2)]
    out = []
    for e in range(2):
        slabs = []
        for start in range(e * HALF, combs[0].shape[0], WIDTH):
            rows = [turned[k][start : start + HALF] for k in range(2)]
            top = jnp.concatenate([rows[0][:, :HALF], rows[1][:, :HALF]], axis=1)
            bottom = jnp.concatenate([rows[0][:, HALF:], rows[1][:, HALF:]], axis=1)
            slabs.append(jnp.concatenate([top, bottom], axis=0))
        out.append(times_left(table[left, e], jnp.concatenate(slabs, axis=1)))
    return out


def butterfly(plane):
    plane = jnp.concatenate([plane[:HALF] + plane[HALF:], plane[:HALF] - plane[HALF:]], axis=0)
    return plane[:, :HALF] + plane[:, HALF:], plane[:, :HALF] - plane[:, HALF:]


def fold(waves):
    parts = [(butterfly(re), butterfly(im)) for re, im in waves]
    return [
        jnp.concatenate([jnp.concatenate([re[e], im[e]], axis=1) for re, im in parts], axis=0) for e in range(2)
    ]


def comb_fields(fields):
    return [
        jnp.concatenate(
            [jnp.concatenate([part[:, e * HALF : (e + 1) * HALF] for part in pair], axis=1) for pair in fields], axis=0
        )
        for e in range(2)
    ]


def plane_of(out, mode, part):
    lanes = slice(mode * WIDTH, (mode + 1) * WIDTH)
    rows = slice(part * HALF, (part + 1) * HALF)
    return [out[e][rows, lanes] for e in range(2)]


def unfold(out):
    def spread(mode, part):
        even, odd = plane_of(out, mode, part)
        plane = jnp.concatenate([even + odd, even - odd], axis=0)
        even, odd = plane[:, :HALF], plane[:, HALF:]
        return jnp.concatenate([even + odd, even - odd], axis=1)

    return [(spread(mode, 0), spread(mode, 1)) for mode in range(out[0].shape[1] // WIDTH)]


def in_combs(out):
    return [tuple(jnp.concatenate(plane_of(out, mode, part), axis=0) for part in range(2)) for mode in range(2)]


def times(a, b):
    return a[0] * b[0] - a[1] * b[1], a[0] * b[1] + a[1] * b[0]


def times_conj(a, b):
    return a[0] * b[0] + a[1] * b[1], a[1] * b[0] - a[0] * b[1]


def iota(axis):
    return lax.broadcasted_iota(jnp.int32, (WIDTH, WIDTH), axis)


def one_hot(condition):
    return jnp.where(condition, 1.0, 0.0).astype(bf16)


def permute(left, planes, right):
    count = len(planes)
    high, low = split(jnp.concatenate(planes, axis=1))
    moved = jnp.dot(left, high, preferred_element_type=f32) + jnp.dot(left, low, preferred_element_type=f32)
    rows = jnp.concatenate([moved[:, k * WIDTH : (k + 1) * WIDTH] for k in range(count)], axis=0)
    high, low = split(rows)
    moved = jnp.dot(high, right, preferred_element_type=f32) + jnp.dot(low, right, preferred_element_type=f32)
    return [moved[k * WIDTH : (k + 1) * WIDTH] for k in range(count)]


MESH_ID = pl.DeviceIdType.MESH


def place():
    row = lax.axis_index("row")
    return row // 16, (row // 2) % 8, lax.axis_index("col"), row % 2


def device(x, y, z, core):
    return ((x * 8 + y) * 2 + core, z)


def start_copy(source, target, sent, landed, to):
    copy = pltpu.make_async_remote_copy(
        src_ref=source, dst_ref=target, send_sem=sent, recv_sem=landed, device_id=to, device_id_type=MESH_ID
    )
    copy.start()
    return copy


def wait_bytes(ref, semaphore):
    pltpu.make_async_copy(ref, ref, semaphore).wait()


class ProbeSum:
    GRAIN = (4, 4, 4, 4, 4, 4, 4, 4)

    def __init__(self, parts, total, from_core, near, from_x, mid, from_y, from_z, sent, landed):
        self.parts, self.total, self.from_core, self.near = parts, total, from_core, near
        self.from_x, self.mid, self.from_y, self.from_z = from_x, mid, from_y, from_z
        self.sent, self.landed = sent, landed
        self.x, self.y, self.z, self.core = place()
        self.arrived = set()

    def x_peers(self):
        return [lax.rem(self.x + d, 4) for d in range(1, 4)]

    def y_peers(self):
        return [lax.rem(self.y + d, 8) for d in range(1, 8)]

    def z_peers(self):
        return [lax.rem(self.z + d, 12) for d in range(1, 12)]

    def cut(self, step, unit):
        grain = self.GRAIN[step]
        if grain == 1:
            return slice(0, 2), slice(0, 256)
        if grain == 2:
            return slice(unit, unit + 1), slice(0, 256)
        return slice(unit // 2, unit // 2 + 1), slice(128 * (unit % 2), 128 * (unit % 2) + 128)

    def volume(self, step, unit):
        modes, lanes = self.cut(step, unit)
        modes, lanes = pl.ds(modes.start, modes.stop - modes.start), pl.ds(lanes.start, lanes.stop - lanes.start)
        if step == 0:
            return self.from_core.at[modes, :, lanes]
        if step == 1:
            return self.from_x.at[:, modes, :, lanes]
        if step == 2:
            return self.from_y.at[:, modes, :, lanes]
        if step == 3:
            return self.from_z.at[pl.ds(0, 11), modes, :, lanes]
        rows = {4: 56, 5: 192, 6: 256}[step]
        return self.total.at[modes, self.core, pl.ds(0, rows), lanes]

    def await_step(self, step, modes, lanes):
        for unit in range(self.GRAIN[step]):
            m, l = self.cut(step, unit)
            apart = m.stop <= modes.start or modes.stop <= m.start or l.stop <= lanes.start or lanes.stop <= l.start
            if not apart and (step, unit) not in self.arrived:
                self.arrived.add((step, unit))
                wait_bytes(self.volume(step, unit), self.landed.at[step, unit])

    def stage(self, step, unit):
        x, y, z, core = self.x, self.y, self.z, self.core
        modes, lanes = self.cut(step, unit)
        if step > 0:
            self.await_step(step - 1, modes, lanes)
        if step == 7:
            return
        m, l = pl.ds(modes.start, modes.stop - modes.start), pl.ds(lanes.start, lanes.stop - lanes.start)
        sent, landed = self.sent.at[step, unit], self.landed.at[step, unit]
        other = device(x, y, z, 1 - core)
        mine = pl.ds(pl.multiple_of(64 * x + 8 * y, 8), 8)
        block = pl.ds(pl.multiple_of(64 * x, 64), 64)
        if step == 0:
            start_copy(self.parts.at[m, 1 - core, :, l], self.from_core.at[m, :, l], sent, landed, other)
        elif step == 1:
            self.near[m, :, l] = self.parts[m, core, :, l] + self.from_core[m, :, l]
            for d, px in enumerate(self.x_peers()):
                rows = pl.ds(pl.multiple_of(64 * px, 64), 64)
                start_copy(self.near.at[m, rows, l], self.from_x.at[d, m, :, l], sent, landed, device(px, y, z, core))
        elif step == 2:
            self.mid[m, :, l] = (self.near[m, block, l] + self.from_x[0, m, :, l]) + (
                self.from_x[1, m, :, l] + self.from_x[2, m, :, l]
            )
            for d, py in enumerate(self.y_peers()):
                rows = pl.ds(pl.multiple_of(8 * py, 8), 8)
                start_copy(self.mid.at[m, rows, l], self.from_y.at[d, m, :, l], sent, landed, device(x, py, z, core))
        elif step == 3:
            piece = self.mid[m, pl.ds(pl.multiple_of(8 * y, 8), 8), l]
            for d in range(7):
                piece = piece + self.from_y[d, m, :, l]
            self.from_z[z, m, :, l] = piece
            spot = self.from_z.at[z, m, :, l]
            for pz in self.z_peers():
                start_copy(spot, spot, sent, landed, device(x, y, pz, core))
        elif step == 4:
            piece = self.from_z[0, m, :, l]
            for d in range(1, 12):
                piece = piece + self.from_z[d, m, :, l]
            self.total[m, core, mine, l] = piece
            spot = self.total.at[m, core, mine, l]
            for py in self.y_peers():
                start_copy(spot, spot, sent, landed, device(x, py, z, core))
        elif step == 5:
            spot = self.total.at[m, core, block, l]
            for px in self.x_peers():
                start_copy(spot, spot, sent, landed, device(px, y, z, core))
        elif step == 6:
            spot = self.total.at[m, core, :, l]
            start_copy(spot, spot, sent, landed, other)

    def stages(self, step):
        for unit in range(self.GRAIN[step]):
            self.stage(step, unit)

    def drain(self):
        for step in range(7):
            for unit in range(self.GRAIN[step]):
                wait_bytes(self.volume(step, unit), self.sent.at[step, unit])

    def greet(self, barrier):
        x, y, z, core = self.x, self.y, self.z, self.core
        peers = [device(x, y, z, 1 - core)]
        peers += [device(px, y, z, core) for px in self.x_peers()]
        peers += [device(x, py, z, core) for py in self.y_peers()]
        peers += [device(x, y, pz, core) for pz in self.z_peers()]
        for peer in peers:
            pl.semaphore_signal(barrier, inc=1, device_id=peer, device_id_type=MESH_ID)
        return len(peers)


PROBE_SUM_SCRATCH = [
    pltpu.VMEM((2, 256, 256), jnp.float32),
    pltpu.VMEM((2, 256, 256), jnp.float32),
    pltpu.VMEM((3, 2, 64, 256), jnp.float32),
    pltpu.VMEM((2, 64, 256), jnp.float32),
    pltpu.VMEM((7, 2, 8, 256), jnp.float32),
    pltpu.VMEM((12, 2, 8, 256), jnp.float32),
    pltpu.SemaphoreType.DMA((7, 4)),
    pltpu.SemaphoreType.DMA((7, 4)),
]


def whole_kernel(
    position, tile_in, probe_in, amplitude_in, table_in,
    grads, down_in, total,
    tile, probe, amplitude, table, loads,
    patch, moved_probe, wave, corner, left_corner, below, merged, side, own_spectrum, side_spectrum, spectrum, sent, landed,
    parts, side_out, side_in, down_out, back_sent, back_landed, *scratch,
):
    def load(source, target, index):
        copy = pltpu.make_async_copy(source, target, loads.at[index])
        copy.start()
        return copy

    row, z = lax.axis_index("row"), lax.axis_index("col")
    core = lax.rem(row, 2)
    up, down = (lax.rem(row + ROWS - 1, ROWS), z), (lax.rem(row + 1, ROWS), z)
    right = (row, lax.rem(z + 1, COLS))
    onward = (row, lax.rem(z + COLS - 1 + 2 * core, COLS))
    back = (row, lax.rem(z + 1 + (COLS - 2) * core, COLS))
    probe_total = ProbeSum(parts, total, *scratch)

    loading = [
        load(source, target, index)
        for index, (source, target) in enumerate(
            [(amplitude_in, amplitude), (tile_in, tile), (probe_in, probe), (table_in, table)]
        )
    ]
    barrier = pltpu.get_barrier_semaphore()
    count = probe_total.greet(barrier)
    for peer in (up, down):
        pl.semaphore_signal(barrier, inc=1, device_id=peer, device_id_type=MESH_ID)

    rows, lanes = iota(0), iota(1)
    first_row = lax.broadcasted_iota(jnp.int32, (8, WIDTH), 0) == 0
    corner[...] = jnp.where(first_row, position[0, 0] - row * WIDTH, position[0, 1] - z * WIDTH)
    to_combs = one_hot(lanes == 2 * lax.rem(rows, HALF) + rows // HALF)
    from_combs = one_hot(rows == 2 * lax.rem(lanes, HALF) + lanes // HALF)
    loading[0].wait()
    own_spectrum[...] = permute(to_combs, [amplitude[...]], from_combs)[0]
    for copy in loading[1:]:
        copy.wait()
    pl.semaphore_wait(barrier, count + 2)

    def chunk(index):
        layer, part, half = index // 4, (index // 2) % 2, index % 2
        return layer, part, pl.ds(half * HALF, HALF)

    copies = [start_copy(corner, left_corner, sent.at[16], landed.at[16], right)]
    for index in range(8):
        spot = chunk(index)
        copies.append(start_copy(tile.at[spot], below.at[spot], sent.at[index], landed.at[index], up))

    @pl.when(core == 1)
    def _():
        start_copy(own_spectrum, side_spectrum, sent.at[17], landed.at[17], right)

    wait_bytes(left_corner, landed.at[16])
    own, other = corner[...], left_corner[...]
    working = own + core * (other - own)
    handing = other + core * (own - other)
    row_start, col_start, hand_start = working[0:1, :], working[1:2, :], handing[0:1, :]
    own_columns = jnp.where(lanes >= col_start, 1, 0) != core

    for index in range(8):
        layer, part, span = chunk(index)
        wait_bytes(below.at[layer, part, span], landed.at[index])
        mine, under = tile[layer, part, span, :], below[layer, part, span, :]
        merged[layer, part, span, :] = jnp.where(rows[span.start : span.start + HALF] >= hand_start, mine, under)
        spot = merged.at[layer, part, span]
        copies.append(start_copy(spot, side.at[layer, part, span], sent.at[8 + index], landed.at[8 + index], onward))
        patch[layer, part, span, :] = jnp.where(rows[span.start : span.start + HALF] >= row_start, mine, under)
        if index == 3:
            shift_rows = one_hot(jnp.bitwise_and(rows - lanes - row_start, WIDTH - 1) == 0)
            shift_cols = one_hot(jnp.bitwise_and(lanes - rows - col_start, WIDTH - 1) == 0)
            planes = [probe[mode, part] for mode in range(2) for part in range(2)]
            for k, plane in enumerate(permute(shift_rows, planes, shift_cols)):
                moved_probe[k // 2, k % 2] = plane

    def patch_of(layer):
        for index in range(4):
            wait_bytes(side.at[chunk(4 * layer + index)], landed.at[8 + 4 * layer + index])
        pair = tuple(jnp.where(own_columns, patch[layer, part], side[layer, part]) for part in range(2))
        patch[layer, 0], patch[layer, 1] = pair
        return pair

    first = patch_of(0)
    waves = [times((moved_probe[mode, 0], moved_probe[mode, 1]), first) for mode in range(2)]
    for mode, pair in enumerate(unfold(both_sides(fold(waves), table, KERNEL))):
        wave[mode, 0], wave[mode, 1] = pair
    second = patch_of(1)

    @pl.when(core == 0)
    def _():
        spectrum[...] = own_spectrum[...]

    @pl.when(core == 1)
    def _():
        wait_bytes(side_spectrum, landed.at[17])
        spectrum[...] = side_spectrum[...]

    waves = [(wave[mode, 0], wave[mode, 1]) for mode in range(2)]
    far = in_combs(both_sides(fold([times(pair, second) for pair in waves]), table, DFT))
    intensity = far[0][0] * far[0][0] + far[0][1] * far[0][1] + (far[1][0] * far[1][0] + far[1][1] * far[1][1])
    weight = 2.0 - 2.0 * spectrum[...] * lax.rsqrt(intensity + intensity_floor)
    far = [(weight * re, weight * im) for re, im in far]
    slope = unfold(both_sides(comb_fields(far), table, DFT_BACK))

    def send_side(layer, terms):
        for part in range(2):
            grads[layer, part] = terms[0][part] + terms[1][part]
            side_out[layer, part] = jnp.where(own_columns, 0.0, grads[layer, part])
        copies.append(
            start_copy(side_out.at[layer], side_in.at[layer], back_sent.at[layer], back_landed.at[layer], back)
        )

    def send_down(layer):
        wait_bytes(side_in.at[layer], back_landed.at[layer])
        for part in range(2):
            mine = jnp.where(own_columns, grads[layer, part], 0.0)
            other = side_in[layer, part]
            down_out[layer, part] = jnp.where(rows < row_start, mine, 0.0) + jnp.where(rows < hand_start, other, 0.0)
            grads[layer, part] = jnp.where(rows < row_start, 0.0, mine) + jnp.where(rows < hand_start, 0.0, other)
        copies.append(
            start_copy(
                down_out.at[layer], down_in.at[layer], back_sent.at[2 + layer], back_landed.at[2 + layer], down
            )
        )

    def finish(layer):
        wait_bytes(down_in.at[layer], back_landed.at[2 + layer])

    send_side(1, [times_conj(slope[mode], waves[mode]) for mode in range(2)])
    shift_rows = one_hot(jnp.bitwise_and(lanes - rows - row_start, WIDTH - 1) == 0)
    shift_cols = one_hot(jnp.bitwise_and(rows - lanes - col_start, WIDTH - 1) == 0)
    first, second = (patch[0, 0], patch[0, 1]), (patch[1, 0], patch[1, 1])
    terms = []
    for mode in range(2):
        bent = unfold(both_sides(fold([times_conj(slope[mode], second)]), table, KERNEL_BACK))[0]
        if mode == 1:
            probe_total.stage(1, 0)
            probe_total.stage(1, 1)
        for part, plane in enumerate(permute(shift_rows, list(times_conj(bent, first)), shift_cols)):
            parts[mode, part] = plane
        probe_total.stage(0, 2 * mode)
        probe_total.stage(0, 2 * mode + 1)
        terms.append(times_conj(bent, (moved_probe[mode, 0], moved_probe[mode, 1])))
    send_side(0, terms)
    probe_total.stage(1, 2)
    probe_total.stage(1, 3)
    send_down(1)
    probe_total.stages(2)
    probe_total.stages(3)
    send_down(0)
    finish(1)
    probe_total.stages(4)
    probe_total.stages(5)
    finish(0)
    probe_total.stages(6)
    probe_total.stages(7)
    probe_total.drain()
    for copy in copies:
        copy.wait_send()

    @pl.when(core == 1)
    def _():
        wait_bytes(side_spectrum, sent.at[17])


def on_device(object_field, probe, scan_positions, amplitudes):
    full, plane = (2, 2, WIDTH, WIDTH), (WIDTH, WIDTH)
    vmem = lambda *dims: pltpu.VMEM(dims, f32)
    anywhere = pl.BlockSpec(memory_space=pltpu.HBM)
    table = jnp.asarray(tables())
    grads, arrived, total = pl.pallas_call(
        whole_kernel,
        out_shape=[jax.ShapeDtypeStruct(full, f32)] * 3,
        in_specs=[pl.BlockSpec(memory_space=pltpu.SMEM)] + [anywhere] * 4,
        out_specs=[pl.BlockSpec(memory_space=pltpu.VMEM)] * 3,
        scratch_shapes=[
            vmem(*full), vmem(*full), vmem(*plane), pltpu.VMEM(table.shape, bf16), pltpu.SemaphoreType.DMA((4,)),
            vmem(*full), vmem(*full), vmem(*full),
            pltpu.VMEM((8, WIDTH), jnp.int32), pltpu.VMEM((8, WIDTH), jnp.int32),
            vmem(*full), vmem(*full), vmem(*full), vmem(*plane), vmem(*plane), vmem(*plane),
            pltpu.SemaphoreType.DMA((18,)), pltpu.SemaphoreType.DMA((18,)),
            vmem(*full), vmem(*full), vmem(*full), vmem(*full),
            pltpu.SemaphoreType.DMA((4,)), pltpu.SemaphoreType.DMA((4,)),
            *PROBE_SUM_SCRATCH,
        ],
        compiler_params=pltpu.CompilerParams(collective_id=0, has_side_effects=True, vmem_limit_bytes=50 << 20),
    )(scan_positions.reshape(1, 2), object_field, probe, amplitudes[0, 0, 0], table)
    return grads + arrived, total * (1.0 / math.sqrt(ROWS * COLS))


def solution(mesh):
    in_specs = (
        P(None, None, "row", "col"),
        P(),
        P("row", "col", None, None),
        P("row", "col", None, None, None),
    )
    out_specs = (P(None, None, "row", "col"), P())
    return jax.shard_map(
        on_device, mesh=mesh, in_specs=in_specs, out_specs=out_specs, check_vma=False
    )
```

```python
import functools
import math

import jax
import jax.numpy as jnp
import ml_dtypes
import numpy as np
from jax import lax
from jax.experimental import pallas as pl
from jax.experimental.pallas import tpu as pltpu
from jax.sharding import PartitionSpec as P

intensity_floor = 0.5
chirp_divisor = 2.0
WIDTH = 256
HALF = 128
ROWS, COLS = 64, 12
f32, bf16 = jnp.float32, jnp.bfloat16


def right_form(matrix):
    return np.block([[matrix.real, matrix.imag], [-matrix.imag, matrix.real]])


def left_form(matrix):
    return np.block([[matrix.real, -matrix.imag], [matrix.imag, matrix.real]])


@functools.lru_cache
def tables():
    indices = np.arange(WIDTH)
    turns = (indices[:, None] * indices[None, :]) % WIDTH
    dft = np.exp(-2j * np.pi * turns / WIDTH) / np.sqrt(WIDTH)
    centered = np.where(indices < HALF, indices, indices - WIDTH).astype(np.float64)
    phase = np.exp(-1j * np.pi * centered**2 / (chirp_divisor * WIDTH))
    kernel = np.conj(dft) @ (phase[:, None] * dft)
    near, far = kernel[:HALF, :HALF], kernel[:HALF, HALF:]
    halves = [(near + far) / 2, (near - far) / 2]
    combs = [dft[:HALF, 0::2], dft[:HALF, 1::2]]
    blocks = np.stack(
        [
            [right_form(m) for m in halves],
            [left_form(m) for m in halves],
            [right_form(m) for m in combs],
            [left_form(m.T) for m in combs],
        ]
    )
    high = blocks.astype(np.float32).astype(ml_dtypes.bfloat16)
    low = (blocks - high.astype(np.float64)).astype(np.float32).astype(ml_dtypes.bfloat16)
    return np.stack([high, low], axis=2)


KERNEL, KERNEL_BACK, DFT, DFT_BACK = (0, 1), (1, 0), (2, 3), (3, 2)


def split(value):
    high = value.astype(bf16)
    return high, (value - high.astype(f32)).astype(bf16)


def times_right(field, table):
    high, low = split(field)
    blocks = jnp.concatenate([table[0], table[0], table[1]], axis=0)
    return jnp.dot(jnp.concatenate([high, low, high], axis=1), blocks, preferred_element_type=f32)


def times_left(table, field):
    high, low = split(field)
    blocks = jnp.concatenate([table[0], table[1], table[0]], axis=1)
    return jnp.dot(blocks, jnp.concatenate([high, high, low], axis=0), preferred_element_type=f32)


def both_sides(combs, table, sides):
    right, left = sides
    turned = [times_right(combs[e], table[right, e]) for e in range(2)]
    out = []
    for e in range(2):
        slabs = []
        for start in range(e * HALF, combs[0].shape[0], WIDTH):
            rows = [turned[k][start : start + HALF] for k in range(2)]
            top = jnp.concatenate([rows[0][:, :HALF], rows[1][:, :HALF]], axis=1)
            bottom = jnp.concatenate([rows[0][:, HALF:], rows[1][:, HALF:]], axis=1)
            slabs.append(jnp.concatenate([top, bottom], axis=0))
        out.append(times_left(table[left, e], jnp.concatenate(slabs, axis=1)))
    return out


def butterfly(plane):
    plane = jnp.concatenate([plane[:HALF] + plane[HALF:], plane[:HALF] - plane[HALF:]], axis=0)
    return plane[:, :HALF] + plane[:, HALF:], plane[:, :HALF] - plane[:, HALF:]


def fold(waves):
    parts = [(butterfly(re), butterfly(im)) for re, im in waves]
    return [
        jnp.concatenate([jnp.concatenate([re[e], im[e]], axis=1) for re, im in parts], axis=0) for e in range(2)
    ]


def comb_fields(fields):
    return [
        jnp.concatenate(
            [jnp.concatenate([part[:, e * HALF : (e + 1) * HALF] for part in pair], axis=1) for pair in fields], axis=0
        )
        for e in range(2)
    ]


def plane_of(out, mode, part):
    lanes = slice(mode * WIDTH, (mode + 1) * WIDTH)
    rows = slice(part * HALF, (part + 1) * HALF)
    return [out[e][rows, lanes] for e in range(2)]


def unfold(out):
    def spread(mode, part):
        even, odd = plane_of(out, mode, part)
        plane = jnp.concatenate([even + odd, even - odd], axis=0)
        even, odd = plane[:, :HALF], plane[:, HALF:]
        return jnp.concatenate([even + odd, even - odd], axis=1)

    return [(spread(mode, 0), spread(mode, 1)) for mode in range(out[0].shape[1] // WIDTH)]


def in_combs(out):
    return [tuple(jnp.concatenate(plane_of(out, mode, part), axis=0) for part in range(2)) for mode in range(2)]


def times(a, b):
    return a[0] * b[0] - a[1] * b[1], a[0] * b[1] + a[1] * b[0]


def times_conj(a, b):
    return a[0] * b[0] + a[1] * b[1], a[1] * b[0] - a[0] * b[1]


def iota(axis):
    return lax.broadcasted_iota(jnp.int32, (WIDTH, WIDTH), axis)


def one_hot(condition):
    return jnp.where(condition, 1.0, 0.0).astype(bf16)


def permute(left, planes, right):
    count = len(planes)
    high, low = split(jnp.concatenate(planes, axis=1))
    moved = jnp.dot(left, high, preferred_element_type=f32) + jnp.dot(left, low, preferred_element_type=f32)
    rows = jnp.concatenate([moved[:, k * WIDTH : (k + 1) * WIDTH] for k in range(count)], axis=0)
    high, low = split(rows)
    moved = jnp.dot(high, right, preferred_element_type=f32) + jnp.dot(low, right, preferred_element_type=f32)
    return [moved[k * WIDTH : (k + 1) * WIDTH] for k in range(count)]


MESH_ID = pl.DeviceIdType.MESH


def place():
    row = lax.axis_index("row")
    return row // 16, (row // 2) % 8, lax.axis_index("col"), row % 2


def device(x, y, z, core):
    return ((x * 8 + y) * 2 + core, z)


def start_copy(source, target, sent, landed, to):
    copy = pltpu.make_async_remote_copy(
        src_ref=source, dst_ref=target, send_sem=sent, recv_sem=landed, device_id=to, device_id_type=MESH_ID
    )
    copy.start()
    return copy


def wait_bytes(ref, semaphore):
    pltpu.make_async_copy(ref, ref, semaphore).wait()


class ProbeSum:
    GRAIN = (4, 4, 4, 4, 4, 4, 4, 4)

    def __init__(self, parts, total, from_core, near, from_x, mid, from_y, from_z, sent, landed):
        self.parts, self.total, self.from_core, self.near = parts, total, from_core, near
        self.from_x, self.mid, self.from_y, self.from_z = from_x, mid, from_y, from_z
        self.sent, self.landed = sent, landed
        self.x, self.y, self.z, self.core = place()
        self.arrived = set()

    def x_peers(self):
        return [lax.rem(self.x + d, 4) for d in range(1, 4)]

    def y_peers(self):
        return [lax.rem(self.y + d, 8) for d in range(1, 8)]

    def z_peers(self):
        return [lax.rem(self.z + d, 12) for d in range(1, 12)]

    def cut(self, step, unit):
        grain = self.GRAIN[step]
        if grain == 1:
            return slice(0, 2), slice(0, 256)
        if grain == 2:
            return slice(unit, unit + 1), slice(0, 256)
        return slice(unit // 2, unit // 2 + 1), slice(128 * (unit % 2), 128 * (unit % 2) + 128)

    def volume(self, step, unit):
        modes, lanes = self.cut(step, unit)
        modes, lanes = pl.ds(modes.start, modes.stop - modes.start), pl.ds(lanes.start, lanes.stop - lanes.start)
        if step == 0:
            return self.from_core.at[modes, :, lanes]
        if step == 1:
            return self.from_x.at[:, modes, :, lanes]
        if step == 2:
            return self.from_y.at[:, modes, :, lanes]
        if step == 3:
            return self.from_z.at[pl.ds(0, 11), modes, :, lanes]
        rows = {4: 56, 5: 192, 6: 256}[step]
        return self.total.at[modes, self.core, pl.ds(0, rows), lanes]

    def await_step(self, step, modes, lanes):
        for unit in range(self.GRAIN[step]):
            m, l = self.cut(step, unit)
            apart = m.stop <= modes.start or modes.stop <= m.start or l.stop <= lanes.start or lanes.stop <= l.start
            if not apart and (step, unit) not in self.arrived:
                self.arrived.add((step, unit))
                wait_bytes(self.volume(step, unit), self.landed.at[step, unit])

    def stage(self, step, unit):
        x, y, z, core = self.x, self.y, self.z, self.core
        modes, lanes = self.cut(step, unit)
        if step > 0:
            self.await_step(step - 1, modes, lanes)
        if step == 7:
            return
        m, l = pl.ds(modes.start, modes.stop - modes.start), pl.ds(lanes.start, lanes.stop - lanes.start)
        sent, landed = self.sent.at[step, unit], self.landed.at[step, unit]
        other = device(x, y, z, 1 - core)
        mine = pl.ds(pl.multiple_of(64 * x + 8 * y, 8), 8)
        block = pl.ds(pl.multiple_of(64 * x, 64), 64)
        if step == 0:
            start_copy(self.parts.at[m, 1 - core, :, l], self.from_core.at[m, :, l], sent, landed, other)
        elif step == 1:
            self.near[m, :, l] = self.parts[m, core, :, l] + self.from_core[m, :, l]
            for d, px in enumerate(self.x_peers()):
                rows = pl.ds(pl.multiple_of(64 * px, 64), 64)
                start_copy(self.near.at[m, rows, l], self.from_x.at[d, m, :, l], sent, landed, device(px, y, z, core))
        elif step == 2:
            self.mid[m, :, l] = (self.near[m, block, l] + self.from_x[0, m, :, l]) + (
                self.from_x[1, m, :, l] + self.from_x[2, m, :, l]
            )
            for d, py in enumerate(self.y_peers()):
                rows = pl.ds(pl.multiple_of(8 * py, 8), 8)
                start_copy(self.mid.at[m, rows, l], self.from_y.at[d, m, :, l], sent, landed, device(x, py, z, core))
        elif step == 3:
            piece = self.mid[m, pl.ds(pl.multiple_of(8 * y, 8), 8), l]
            for d in range(7):
                piece = piece + self.from_y[d, m, :, l]
            self.from_z[z, m, :, l] = piece
            spot = self.from_z.at[z, m, :, l]
            for pz in self.z_peers():
                start_copy(spot, spot, sent, landed, device(x, y, pz, core))
        elif step == 4:
            piece = self.from_z[0, m, :, l]
            for d in range(1, 12):
                piece = piece + self.from_z[d, m, :, l]
            self.total[m, core, mine, l] = piece * (1.0 / math.sqrt(ROWS * COLS))
            spot = self.total.at[m, core, mine, l]
            for py in self.y_peers():
                start_copy(spot, spot, sent, landed, device(x, py, z, core))
        elif step == 5:
            spot = self.total.at[m, core, block, l]
            for px in self.x_peers():
                start_copy(spot, spot, sent, landed, device(px, y, z, core))
        elif step == 6:
            spot = self.total.at[m, core, :, l]
            start_copy(spot, spot, sent, landed, other)

    def stages(self, step):
        for unit in range(self.GRAIN[step]):
            self.stage(step, unit)

    def drain(self):
        for step in range(7):
            for unit in range(self.GRAIN[step]):
                wait_bytes(self.volume(step, unit), self.sent.at[step, unit])

    def greet(self, barrier):
        x, y, z, core = self.x, self.y, self.z, self.core
        peers = [device(x, y, z, 1 - core)]
        peers += [device(px, y, z, core) for px in self.x_peers()]
        peers += [device(x, py, z, core) for py in self.y_peers()]
        peers += [device(x, y, pz, core) for pz in self.z_peers()]
        for peer in peers:
            pl.semaphore_signal(barrier, inc=1, device_id=peer, device_id_type=MESH_ID)
        return len(peers)


PROBE_SUM_SCRATCH = [
    pltpu.VMEM((2, 256, 256), jnp.float32),
    pltpu.VMEM((2, 256, 256), jnp.float32),
    pltpu.VMEM((3, 2, 64, 256), jnp.float32),
    pltpu.VMEM((2, 64, 256), jnp.float32),
    pltpu.VMEM((7, 2, 8, 256), jnp.float32),
    pltpu.VMEM((12, 2, 8, 256), jnp.float32),
    pltpu.SemaphoreType.DMA((7, 4)),
    pltpu.SemaphoreType.DMA((7, 4)),
]


def whole_kernel(
    position, tile_in, probe_in, amplitude_in, table_in,
    grads, down_in, total,
    tile, probe, amplitude, table, loads,
    patch, moved_probe, wave, corner, left_corner, below, merged, side, own_spectrum, side_spectrum, spectrum, sent, landed,
    parts, side_out, side_in, down_out, back_sent, back_landed, *scratch,
):
    def load(source, target, index):
        copy = pltpu.make_async_copy(source, target, loads.at[index])
        copy.start()
        return copy

    row, z = lax.axis_index("row"), lax.axis_index("col")
    core = lax.rem(row, 2)
    up, down = (lax.rem(row + ROWS - 1, ROWS), z), (lax.rem(row + 1, ROWS), z)
    right = (row, lax.rem(z + 1, COLS))
    onward = (row, lax.rem(z + COLS - 1 + 2 * core, COLS))
    back = (row, lax.rem(z + 1 + (COLS - 2) * core, COLS))
    probe_total = ProbeSum(parts, total, *scratch)

    loading = [
        load(source, target, index)
        for index, (source, target) in enumerate(
            [(amplitude_in, amplitude), (tile_in, tile), (probe_in, probe), (table_in, table)]
        )
    ]
    barrier = pltpu.get_barrier_semaphore()
    count = probe_total.greet(barrier)
    for peer in (up, down):
        pl.semaphore_signal(barrier, inc=1, device_id=peer, device_id_type=MESH_ID)

    rows, lanes = iota(0), iota(1)
    first_row = lax.broadcasted_iota(jnp.int32, (8, WIDTH), 0) == 0
    corner[...] = jnp.where(first_row, position[0, 0] - row * WIDTH, position[0, 1] - z * WIDTH)
    to_combs = one_hot(lanes == 2 * lax.rem(rows, HALF) + rows // HALF)
    from_combs = one_hot(rows == 2 * lax.rem(lanes, HALF) + lanes // HALF)
    loading[0].wait()
    own_spectrum[...] = permute(to_combs, [amplitude[...]], from_combs)[0]
    for copy in loading[1:]:
        copy.wait()
    pl.semaphore_wait(barrier, count + 2)

    def chunk(index):
        layer, part, half = index // 4, (index // 2) % 2, index % 2
        return layer, part, pl.ds(half * HALF, HALF)

    copies = [start_copy(corner, left_corner, sent.at[16], landed.at[16], right)]
    for index in range(8):
        spot = chunk(index)
        copies.append(start_copy(tile.at[spot], below.at[spot], sent.at[index], landed.at[index], up))

    @pl.when(core == 1)
    def _():
        start_copy(own_spectrum, side_spectrum, sent.at[17], landed.at[17], right)

    wait_bytes(left_corner, landed.at[16])
    own, other = corner[...], left_corner[...]
    working = own + core * (other - own)
    handing = other + core * (own - other)
    row_start, col_start, hand_start = working[0:1, :], working[1:2, :], handing[0:1, :]
    own_columns = jnp.where(lanes >= col_start, 1, 0) != core

    for index in range(8):
        layer, part, span = chunk(index)
        wait_bytes(below.at[layer, part, span], landed.at[index])
        mine, under = tile[layer, part, span, :], below[layer, part, span, :]
        merged[layer, part, span, :] = jnp.where(rows[span.start : span.start + HALF] >= hand_start, mine, under)
        spot = merged.at[layer, part, span]
        copies.append(start_copy(spot, side.at[layer, part, span], sent.at[8 + index], landed.at[8 + index], onward))
        patch[layer, part, span, :] = jnp.where(rows[span.start : span.start + HALF] >= row_start, mine, under)
        if index == 3:
            shift_rows = one_hot(jnp.bitwise_and(rows - lanes - row_start, WIDTH - 1) == 0)
            shift_cols = one_hot(jnp.bitwise_and(lanes - rows - col_start, WIDTH - 1) == 0)
            planes = [probe[mode, part] for mode in range(2) for part in range(2)]
            for k, plane in enumerate(permute(shift_rows, planes, shift_cols)):
                moved_probe[k // 2, k % 2] = plane

    def patch_of(layer):
        for index in range(4):
            wait_bytes(side.at[chunk(4 * layer + index)], landed.at[8 + 4 * layer + index])
        pair = tuple(jnp.where(own_columns, patch[layer, part], side[layer, part]) for part in range(2))
        patch[layer, 0], patch[layer, 1] = pair
        return pair

    first = patch_of(0)
    waves = [times((moved_probe[mode, 0], moved_probe[mode, 1]), first) for mode in range(2)]
    for mode, pair in enumerate(unfold(both_sides(fold(waves), table, KERNEL))):
        wave[mode, 0], wave[mode, 1] = pair
    second = patch_of(1)

    @pl.when(core == 0)
    def _():
        spectrum[...] = own_spectrum[...]

    @pl.when(core == 1)
    def _():
        wait_bytes(side_spectrum, landed.at[17])
        spectrum[...] = side_spectrum[...]

    waves = [(wave[mode, 0], wave[mode, 1]) for mode in range(2)]
    far = in_combs(both_sides(fold([times(pair, second) for pair in waves]), table, DFT))
    intensity = far[0][0] * far[0][0] + far[0][1] * far[0][1] + (far[1][0] * far[1][0] + far[1][1] * far[1][1])
    weight = 2.0 - 2.0 * spectrum[...] * lax.rsqrt(intensity + intensity_floor)
    far = [(weight * re, weight * im) for re, im in far]
    slope = unfold(both_sides(comb_fields(far), table, DFT_BACK))

    def send_side(layer, terms):
        for part in range(2):
            grads[layer, part] = terms[0][part] + terms[1][part]
            side_out[layer, part] = jnp.where(own_columns, 0.0, grads[layer, part])
        copies.append(
            start_copy(side_out.at[layer], side_in.at[layer], back_sent.at[layer], back_landed.at[layer], back)
        )

    def send_down(layer):
        wait_bytes(side_in.at[layer], back_landed.at[layer])
        for part in range(2):
            mine = jnp.where(own_columns, grads[layer, part], 0.0)
            other = side_in[layer, part]
            down_out[layer, part] = jnp.where(rows < row_start, mine, 0.0) + jnp.where(rows < hand_start, other, 0.0)
            grads[layer, part] = jnp.where(rows < row_start, 0.0, mine) + jnp.where(rows < hand_start, 0.0, other)
        copies.append(
            start_copy(
                down_out.at[layer], down_in.at[layer], back_sent.at[2 + layer], back_landed.at[2 + layer], down
            )
        )

    def finish(layer):
        wait_bytes(down_in.at[layer], back_landed.at[2 + layer])

    send_side(1, [times_conj(slope[mode], waves[mode]) for mode in range(2)])
    shift_rows = one_hot(jnp.bitwise_and(lanes - rows - row_start, WIDTH - 1) == 0)
    shift_cols = one_hot(jnp.bitwise_and(rows - lanes - col_start, WIDTH - 1) == 0)
    first, second = (patch[0, 0], patch[0, 1]), (patch[1, 0], patch[1, 1])
    terms = []
    for mode in range(2):
        bent = unfold(both_sides(fold([times_conj(slope[mode], second)]), table, KERNEL_BACK))[0]
        if mode == 1:
            probe_total.stage(1, 0)
            probe_total.stage(1, 1)
        for part, plane in enumerate(permute(shift_rows, list(times_conj(bent, first)), shift_cols)):
            parts[mode, part] = plane
        probe_total.stage(0, 2 * mode)
        probe_total.stage(0, 2 * mode + 1)
        terms.append(times_conj(bent, (moved_probe[mode, 0], moved_probe[mode, 1])))
    send_side(0, terms)
    probe_total.stage(1, 2)
    probe_total.stage(1, 3)
    probe_total.stages(2)
    send_down(1)
    probe_total.stages(3)
    send_down(0)
    finish(1)
    probe_total.stages(4)
    probe_total.stages(5)
    finish(0)
    probe_total.stages(6)
    probe_total.stages(7)
    probe_total.drain()
    for copy in copies:
        copy.wait_send()

    @pl.when(core == 1)
    def _():
        wait_bytes(side_spectrum, sent.at[17])


def last_kernel(grads, arrived, total, object_gradient, probe_gradient, summed, written):
    copies = []

    def write(source, target):
        copies.append(pltpu.make_async_copy(source, target, written.at[len(copies)]))
        copies[-1].start()

    spots = [(first, second) for first in range(2) for second in range(2)]
    for spot in spots:
        write(total.at[spot], probe_gradient.at[spot])
    for spot in spots:
        summed[spot] = grads[spot] + arrived[spot]
        write(summed.at[spot], object_gradient.at[spot])
    for copy in copies:
        copy.wait()


def on_device(object_field, probe, scan_positions, amplitudes):
    full, plane = (2, 2, WIDTH, WIDTH), (WIDTH, WIDTH)
    vmem = lambda *dims: pltpu.VMEM(dims, f32)
    anywhere = pl.BlockSpec(memory_space=pltpu.HBM)
    table = jnp.asarray(tables())
    operands = (scan_positions.reshape(1, 2), object_field, probe, amplitudes[0, 0, 0], table)
    grads, arrived, total = pl.pallas_call(
        whole_kernel,
        out_shape=[jax.ShapeDtypeStruct(full, f32)] * 3,
        in_specs=[pl.BlockSpec(memory_space=pltpu.SMEM)] + [anywhere] * 4,
        out_specs=[pl.BlockSpec(memory_space=pltpu.VMEM)] * 3,
        scratch_shapes=[
            vmem(*full), vmem(*full), vmem(*plane), pltpu.VMEM(table.shape, bf16), pltpu.SemaphoreType.DMA((4,)),
            vmem(*full), vmem(*full), vmem(*full),
            pltpu.VMEM((8, WIDTH), jnp.int32), pltpu.VMEM((8, WIDTH), jnp.int32),
            vmem(*full), vmem(*full), vmem(*full), vmem(*plane), vmem(*plane), vmem(*plane),
            pltpu.SemaphoreType.DMA((18,)), pltpu.SemaphoreType.DMA((18,)),
            vmem(*full), vmem(*full), vmem(*full), vmem(*full),
            pltpu.SemaphoreType.DMA((4,)), pltpu.SemaphoreType.DMA((4,)),
            *PROBE_SUM_SCRATCH,
        ],
        compiler_params=pltpu.CompilerParams(collective_id=0, has_side_effects=True, vmem_limit_bytes=40 << 20),
    )(*(pltpu.with_memory_space_constraint(x, pltpu.HBM) for x in operands))
    return tuple(
        pl.pallas_call(
            last_kernel,
            out_shape=[jax.ShapeDtypeStruct(full, f32)] * 2,
            in_specs=[pl.BlockSpec(memory_space=pltpu.VMEM)] * 3,
            out_specs=[anywhere] * 2,
            scratch_shapes=[vmem(*full), pltpu.SemaphoreType.DMA((8,))],
            compiler_params=pltpu.CompilerParams(vmem_limit_bytes=8 << 20),
        )(grads, arrived, total)
    )


def solution(mesh):
    in_specs = (
        P(None, None, "row", "col"),
        P(),
        P("row", "col", None, None),
        P("row", "col", None, None, None),
    )
    out_specs = (P(None, None, "row", "col"), P())
    return jax.shard_map(
        on_device, mesh=mesh, in_specs=in_specs, out_specs=out_specs, check_vma=False
    )
```

```python
import functools
import math

import jax
import jax.numpy as jnp
import ml_dtypes
import numpy as np
from jax import lax
from jax.experimental import pallas as pl
from jax.experimental.pallas import tpu as pltpu
from jax.sharding import PartitionSpec as P

intensity_floor = 0.5
chirp_divisor = 2.0
WIDTH = 256
HALF = 128
ROWS, COLS = 64, 12
f32, bf16 = jnp.float32, jnp.bfloat16


def right_form(matrix):
    return np.block([[matrix.real, matrix.imag], [-matrix.imag, matrix.real]])


def left_form(matrix):
    return np.block([[matrix.real, -matrix.imag], [matrix.imag, matrix.real]])


@functools.lru_cache
def tables():
    indices = np.arange(WIDTH)
    turns = (indices[:, None] * indices[None, :]) % WIDTH
    dft = np.exp(-2j * np.pi * turns / WIDTH) / np.sqrt(WIDTH)
    centered = np.where(indices < HALF, indices, indices - WIDTH).astype(np.float64)
    phase = np.exp(-1j * np.pi * centered**2 / (chirp_divisor * WIDTH))
    kernel = np.conj(dft) @ (phase[:, None] * dft)
    near, far = kernel[:HALF, :HALF], kernel[:HALF, HALF:]
    halves = [(near + far) / 2, (near - far) / 2]
    combs = [dft[:HALF, 0::2], dft[:HALF, 1::2]]
    blocks = np.stack(
        [
            [right_form(m) for m in halves],
            [left_form(m) for m in halves],
            [right_form(m) for m in combs],
            [left_form(m.T) for m in combs],
        ]
    )
    high = blocks.astype(np.float32).astype(ml_dtypes.bfloat16)
    low = (blocks - high.astype(np.float64)).astype(np.float32).astype(ml_dtypes.bfloat16)
    return np.stack([high, low], axis=2)


KERNEL, KERNEL_BACK, DFT, DFT_BACK = (0, 1), (1, 0), (2, 3), (3, 2)


def split(value):
    high = value.astype(bf16)
    return high, (value - high.astype(f32)).astype(bf16)


def times_right(field, table):
    high, low = split(field)
    blocks = jnp.concatenate([table[0], table[0], table[1]], axis=0)
    return jnp.dot(jnp.concatenate([high, low, high], axis=1), blocks, preferred_element_type=f32)


def times_left(table, field):
    high, low = split(field)
    blocks = jnp.concatenate([table[0], table[1], table[0]], axis=1)
    return jnp.dot(blocks, jnp.concatenate([high, high, low], axis=0), preferred_element_type=f32)


def both_sides(combs, table, sides):
    right, left = sides
    turned = [times_right(combs[e], table[right, e]) for e in range(2)]
    out = []
    for e in range(2):
        slabs = []
        for start in range(e * HALF, combs[0].shape[0], WIDTH):
            rows = [turned[k][start : start + HALF] for k in range(2)]
            top = jnp.concatenate([rows[0][:, :HALF], rows[1][:, :HALF]], axis=1)
            bottom = jnp.concatenate([rows[0][:, HALF:], rows[1][:, HALF:]], axis=1)
            slabs.append(jnp.concatenate([top, bottom], axis=0))
        out.append(times_left(table[left, e], jnp.concatenate(slabs, axis=1)))
    return out


def butterfly(plane):
    plane = jnp.concatenate([plane[:HALF] + plane[HALF:], plane[:HALF] - plane[HALF:]], axis=0)
    return plane[:, :HALF] + plane[:, HALF:], plane[:, :HALF] - plane[:, HALF:]


def fold(waves):
    parts = [(butterfly(re), butterfly(im)) for re, im in waves]
    return [
        jnp.concatenate([jnp.concatenate([re[e], im[e]], axis=1) for re, im in parts], axis=0) for e in range(2)
    ]


def comb_fields(fields):
    return [
        jnp.concatenate(
            [jnp.concatenate([part[:, e * HALF : (e + 1) * HALF] for part in pair], axis=1) for pair in fields], axis=0
        )
        for e in range(2)
    ]


def plane_of(out, mode, part):
    lanes = slice(mode * WIDTH, (mode + 1) * WIDTH)
    rows = slice(part * HALF, (part + 1) * HALF)
    return [out[e][rows, lanes] for e in range(2)]


def unfold(out):
    def spread(mode, part):
        even, odd = plane_of(out, mode, part)
        plane = jnp.concatenate([even + odd, even - odd], axis=0)
        even, odd = plane[:, :HALF], plane[:, HALF:]
        return jnp.concatenate([even + odd, even - odd], axis=1)

    return [(spread(mode, 0), spread(mode, 1)) for mode in range(out[0].shape[1] // WIDTH)]


def in_combs(out):
    return [tuple(jnp.concatenate(plane_of(out, mode, part), axis=0) for part in range(2)) for mode in range(2)]


def times(a, b):
    return a[0] * b[0] - a[1] * b[1], a[0] * b[1] + a[1] * b[0]


def times_conj(a, b):
    return a[0] * b[0] + a[1] * b[1], a[1] * b[0] - a[0] * b[1]


def iota(axis):
    return lax.broadcasted_iota(jnp.int32, (WIDTH, WIDTH), axis)


def one_hot(condition):
    return jnp.where(condition, 1.0, 0.0).astype(bf16)


def permute(left, planes, right):
    count = len(planes)
    high, low = split(jnp.concatenate(planes, axis=1))
    moved = jnp.dot(left, high, preferred_element_type=f32) + jnp.dot(left, low, preferred_element_type=f32)
    rows = jnp.concatenate([moved[:, k * WIDTH : (k + 1) * WIDTH] for k in range(count)], axis=0)
    high, low = split(rows)
    moved = jnp.dot(high, right, preferred_element_type=f32) + jnp.dot(low, right, preferred_element_type=f32)
    return [moved[k * WIDTH : (k + 1) * WIDTH] for k in range(count)]


MESH_ID = pl.DeviceIdType.MESH


def place():
    row = lax.axis_index("row")
    return row // 16, (row // 2) % 8, lax.axis_index("col"), row % 2


def device(x, y, z, core):
    return ((x * 8 + y) * 2 + core, z)


def start_copy(source, target, sent, landed, to):
    copy = pltpu.make_async_remote_copy(
        src_ref=source, dst_ref=target, send_sem=sent, recv_sem=landed, device_id=to, device_id_type=MESH_ID
    )
    copy.start()
    return copy


def wait_bytes(ref, semaphore):
    pltpu.make_async_copy(ref, ref, semaphore).wait()


class ProbeSum:
    GRAIN = (4, 4, 4, 4, 4, 4, 4, 4)

    def __init__(self, parts, total, from_core, near, from_x, mid, from_y, from_z, sent, landed):
        self.parts, self.total, self.from_core, self.near = parts, total, from_core, near
        self.from_x, self.mid, self.from_y, self.from_z = from_x, mid, from_y, from_z
        self.sent, self.landed = sent, landed
        self.x, self.y, self.z, self.core = place()
        self.arrived = set()

    def x_peers(self):
        return [lax.rem(self.x + d, 4) for d in range(1, 4)]

    def y_peers(self):
        return [lax.rem(self.y + d, 8) for d in range(1, 8)]

    def z_peers(self):
        return [lax.rem(self.z + d, 12) for d in range(1, 12)]

    def cut(self, step, unit):
        grain = self.GRAIN[step]
        if grain == 1:
            return slice(0, 2), slice(0, 256)
        if grain == 2:
            return slice(unit, unit + 1), slice(0, 256)
        return slice(unit // 2, unit // 2 + 1), slice(128 * (unit % 2), 128 * (unit % 2) + 128)

    def volume(self, step, unit):
        modes, lanes = self.cut(step, unit)
        modes, lanes = pl.ds(modes.start, modes.stop - modes.start), pl.ds(lanes.start, lanes.stop - lanes.start)
        if step == 0:
            return self.from_core.at[modes, :, lanes]
        if step == 1:
            return self.from_x.at[:, modes, :, lanes]
        if step == 2:
            return self.from_y.at[:, modes, :, lanes]
        if step == 3:
            return self.from_z.at[pl.ds(0, 11), modes, :, lanes]
        rows = {4: 56, 5: 192, 6: 256}[step]
        return self.total.at[modes, self.core, pl.ds(0, rows), lanes]

    def await_step(self, step, modes, lanes):
        for unit in range(self.GRAIN[step]):
            m, l = self.cut(step, unit)
            apart = m.stop <= modes.start or modes.stop <= m.start or l.stop <= lanes.start or lanes.stop <= l.start
            if not apart and (step, unit) not in self.arrived:
                self.arrived.add((step, unit))
                wait_bytes(self.volume(step, unit), self.landed.at[step, unit])

    def stage(self, step, unit):
        x, y, z, core = self.x, self.y, self.z, self.core
        modes, lanes = self.cut(step, unit)
        if step > 0:
            self.await_step(step - 1, modes, lanes)
        if step == 7:
            return
        m, l = pl.ds(modes.start, modes.stop - modes.start), pl.ds(lanes.start, lanes.stop - lanes.start)
        sent, landed = self.sent.at[step, unit], self.landed.at[step, unit]
        other = device(x, y, z, 1 - core)
        mine = pl.ds(pl.multiple_of(64 * x + 8 * y, 8), 8)
        block = pl.ds(pl.multiple_of(64 * x, 64), 64)
        if step == 0:
            start_copy(self.parts.at[m, 1 - core, :, l], self.from_core.at[m, :, l], sent, landed, other)
        elif step == 1:
            self.near[m, :, l] = self.parts[m, core, :, l] + self.from_core[m, :, l]
            for d, px in enumerate(self.x_peers()):
                rows = pl.ds(pl.multiple_of(64 * px, 64), 64)
                start_copy(self.near.at[m, rows, l], self.from_x.at[d, m, :, l], sent, landed, device(px, y, z, core))
        elif step == 2:
            self.mid[m, :, l] = (self.near[m, block, l] + self.from_x[0, m, :, l]) + (
                self.from_x[1, m, :, l] + self.from_x[2, m, :, l]
            )
            for d, py in enumerate(self.y_peers()):
                rows = pl.ds(pl.multiple_of(8 * py, 8), 8)
                start_copy(self.mid.at[m, rows, l], self.from_y.at[d, m, :, l], sent, landed, device(x, py, z, core))
        elif step == 3:
            piece = self.mid[m, pl.ds(pl.multiple_of(8 * y, 8), 8), l]
            for d in range(7):
                piece = piece + self.from_y[d, m, :, l]
            self.from_z[z, m, :, l] = piece
            spot = self.from_z.at[z, m, :, l]
            for pz in self.z_peers():
                start_copy(spot, spot, sent, landed, device(x, y, pz, core))
        elif step == 4:
            piece = self.from_z[0, m, :, l]
            for d in range(1, 12):
                piece = piece + self.from_z[d, m, :, l]
            self.total[m, core, mine, l] = piece * (1.0 / math.sqrt(ROWS * COLS))
            spot = self.total.at[m, core, mine, l]
            for py in self.y_peers():
                start_copy(spot, spot, sent, landed, device(x, py, z, core))
        elif step == 5:
            spot = self.total.at[m, core, block, l]
            for px in self.x_peers():
                start_copy(spot, spot, sent, landed, device(px, y, z, core))
        elif step == 6:
            spot = self.total.at[m, core, :, l]
            start_copy(spot, spot, sent, landed, other)

    def stages(self, step):
        for unit in range(self.GRAIN[step]):
            self.stage(step, unit)

    def drain(self):
        for step in range(7):
            for unit in range(self.GRAIN[step]):
                wait_bytes(self.volume(step, unit), self.sent.at[step, unit])

    REACH = (2, 4, 6)

    def beside(self, axis, by):
        x, y, z, core = self.x, self.y, self.z, self.core
        if axis == 0:
            return device(lax.rem(x + 4 + by, 4), y, z, core)
        if axis == 1:
            return device(x, lax.rem(y + 8 + by, 8), z, core)
        return device(x, y, lax.rem(z + 12 + by, 12), core)

    def greet(self, barrier):
        peers = [device(self.x, self.y, self.z, 1 - self.core)]
        peers += [self.beside(axis, by) for axis in range(3) for by in (1, -1)]
        for peer in peers:
            pl.semaphore_signal(barrier, inc=1, device_id=peer, device_id_type=MESH_ID)
        return len(peers)

    def pass_word(self, words, distance):
        for axis, reach in enumerate(self.REACH):
            for way, by in enumerate((1, -1)):
                if 2 < distance <= reach + 1:
                    pl.semaphore_wait(words.at[axis, way, distance - 3], 1)
                if distance <= reach:
                    word = words.at[axis, way, distance - 2]
                    pl.semaphore_signal(word, inc=1, device_id=self.beside(axis, by), device_id_type=MESH_ID)


PROBE_SUM_SCRATCH = [
    pltpu.VMEM((2, 256, 256), jnp.float32),
    pltpu.VMEM((2, 256, 256), jnp.float32),
    pltpu.VMEM((3, 2, 64, 256), jnp.float32),
    pltpu.VMEM((2, 64, 256), jnp.float32),
    pltpu.VMEM((7, 2, 8, 256), jnp.float32),
    pltpu.VMEM((12, 2, 8, 256), jnp.float32),
    pltpu.SemaphoreType.DMA((7, 4)),
    pltpu.SemaphoreType.DMA((7, 4)),
]


def whole_kernel(
    position, tile_in, probe_in, amplitude_in, table_in,
    grads, down_in, total,
    tile, probe, amplitude, table, loads,
    patch, moved_probe, wave, corner, left_corner, below, merged, side, own_spectrum, side_spectrum, spectrum, sent, landed, words,
    parts, side_out, side_in, down_out, back_sent, back_landed, *scratch,
):
    def load(source, target, index):
        copy = pltpu.make_async_copy(source, target, loads.at[index])
        copy.start()
        return copy

    row, z = lax.axis_index("row"), lax.axis_index("col")
    core = lax.rem(row, 2)
    up, down = (lax.rem(row + ROWS - 1, ROWS), z), (lax.rem(row + 1, ROWS), z)
    right = (row, lax.rem(z + 1, COLS))
    onward = (row, lax.rem(z + COLS - 1 + 2 * core, COLS))
    back = (row, lax.rem(z + 1 + (COLS - 2) * core, COLS))
    probe_total = ProbeSum(parts, total, *scratch)

    loading = [
        load(source, target, index)
        for index, (source, target) in enumerate(
            [(amplitude_in, amplitude), (tile_in, tile), (probe_in, probe), (table_in, table)]
        )
    ]
    barrier = pltpu.get_barrier_semaphore()
    count = probe_total.greet(barrier)
    for peer in (up, down):
        pl.semaphore_signal(barrier, inc=1, device_id=peer, device_id_type=MESH_ID)

    rows, lanes = iota(0), iota(1)
    first_row = lax.broadcasted_iota(jnp.int32, (8, WIDTH), 0) == 0
    corner[...] = jnp.where(first_row, position[0, 0] - row * WIDTH, position[0, 1] - z * WIDTH)
    to_combs = one_hot(lanes == 2 * lax.rem(rows, HALF) + rows // HALF)
    from_combs = one_hot(rows == 2 * lax.rem(lanes, HALF) + lanes // HALF)
    loading[0].wait()
    own_spectrum[...] = permute(to_combs, [amplitude[...]], from_combs)[0]
    for copy in loading[1:]:
        copy.wait()
    pl.semaphore_wait(barrier, count + 2)

    def chunk(index):
        layer, part, half = index // 4, (index // 2) % 2, index % 2
        return layer, part, pl.ds(half * HALF, HALF)

    copies = [start_copy(corner, left_corner, sent.at[16], landed.at[16], right)]
    for index in range(8):
        spot = chunk(index)
        copies.append(start_copy(tile.at[spot], below.at[spot], sent.at[index], landed.at[index], up))

    @pl.when(core == 1)
    def _():
        start_copy(own_spectrum, side_spectrum, sent.at[17], landed.at[17], right)

    probe_total.pass_word(words, 2)
    wait_bytes(left_corner, landed.at[16])
    own, other = corner[...], left_corner[...]
    working = own + core * (other - own)
    handing = other + core * (own - other)
    row_start, col_start, hand_start = working[0:1, :], working[1:2, :], handing[0:1, :]
    own_columns = jnp.where(lanes >= col_start, 1, 0) != core

    for index in range(8):
        layer, part, span = chunk(index)
        wait_bytes(below.at[layer, part, span], landed.at[index])
        mine, under = tile[layer, part, span, :], below[layer, part, span, :]
        merged[layer, part, span, :] = jnp.where(rows[span.start : span.start + HALF] >= hand_start, mine, under)
        spot = merged.at[layer, part, span]
        copies.append(start_copy(spot, side.at[layer, part, span], sent.at[8 + index], landed.at[8 + index], onward))
        patch[layer, part, span, :] = jnp.where(rows[span.start : span.start + HALF] >= row_start, mine, under)
        if index % 2:
            probe_total.pass_word(words, 3 + index // 2)
        if index == 3:
            shift_rows = one_hot(jnp.bitwise_and(rows - lanes - row_start, WIDTH - 1) == 0)
            shift_cols = one_hot(jnp.bitwise_and(lanes - rows - col_start, WIDTH - 1) == 0)
            planes = [probe[mode, part] for mode in range(2) for part in range(2)]
            for k, plane in enumerate(permute(shift_rows, planes, shift_cols)):
                moved_probe[k // 2, k % 2] = plane

    def patch_of(layer):
        for index in range(4):
            wait_bytes(side.at[chunk(4 * layer + index)], landed.at[8 + 4 * layer + index])
        pair = tuple(jnp.where(own_columns, patch[layer, part], side[layer, part]) for part in range(2))
        patch[layer, 0], patch[layer, 1] = pair
        return pair

    first = patch_of(0)
    waves = [times((moved_probe[mode, 0], moved_probe[mode, 1]), first) for mode in range(2)]
    for mode, pair in enumerate(unfold(both_sides(fold(waves), table, KERNEL))):
        wave[mode, 0], wave[mode, 1] = pair
    probe_total.pass_word(words, 7)
    second = patch_of(1)

    @pl.when(core == 0)
    def _():
        spectrum[...] = own_spectrum[...]

    @pl.when(core == 1)
    def _():
        wait_bytes(side_spectrum, landed.at[17])
        spectrum[...] = side_spectrum[...]

    waves = [(wave[mode, 0], wave[mode, 1]) for mode in range(2)]
    far = in_combs(both_sides(fold([times(pair, second) for pair in waves]), table, DFT))
    intensity = far[0][0] * far[0][0] + far[0][1] * far[0][1] + (far[1][0] * far[1][0] + far[1][1] * far[1][1])
    weight = 2.0 - 2.0 * spectrum[...] * lax.rsqrt(intensity + intensity_floor)
    far = [(weight * re, weight * im) for re, im in far]
    slope = unfold(both_sides(comb_fields(far), table, DFT_BACK))

    def send_side(layer, terms):
        for part in range(2):
            grads[layer, part] = terms[0][part] + terms[1][part]
            side_out[layer, part] = jnp.where(own_columns, 0.0, grads[layer, part])
        copies.append(
            start_copy(side_out.at[layer], side_in.at[layer], back_sent.at[layer], back_landed.at[layer], back)
        )

    def send_down(layer):
        wait_bytes(side_in.at[layer], back_landed.at[layer])
        for part in range(2):
            mine = jnp.where(own_columns, grads[layer, part], 0.0)
            other = side_in[layer, part]
            down_out[layer, part] = jnp.where(rows < row_start, mine, 0.0) + jnp.where(rows < hand_start, other, 0.0)
            grads[layer, part] = jnp.where(rows < row_start, 0.0, mine) + jnp.where(rows < hand_start, 0.0, other)
        copies.append(
            start_copy(
                down_out.at[layer], down_in.at[layer], back_sent.at[2 + layer], back_landed.at[2 + layer], down
            )
        )

    def finish(layer):
        wait_bytes(down_in.at[layer], back_landed.at[2 + layer])

    send_side(1, [times_conj(slope[mode], waves[mode]) for mode in range(2)])
    shift_rows = one_hot(jnp.bitwise_and(lanes - rows - row_start, WIDTH - 1) == 0)
    shift_cols = one_hot(jnp.bitwise_and(rows - lanes - col_start, WIDTH - 1) == 0)
    first, second = (patch[0, 0], patch[0, 1]), (patch[1, 0], patch[1, 1])
    terms = []
    for mode in range(2):
        bent = unfold(both_sides(fold([times_conj(slope[mode], second)]), table, KERNEL_BACK))[0]
        if mode == 1:
            probe_total.stage(1, 0)
            probe_total.stage(1, 1)
        for part, plane in enumerate(permute(shift_rows, list(times_conj(bent, first)), shift_cols)):
            parts[mode, part] = plane
        probe_total.stage(0, 2 * mode)
        probe_total.stage(0, 2 * mode + 1)
        terms.append(times_conj(bent, (moved_probe[mode, 0], moved_probe[mode, 1])))
    send_side(0, terms)
    probe_total.stage(1, 2)
    probe_total.stage(1, 3)
    probe_total.stages(2)
    send_down(1)
    probe_total.stages(3)
    send_down(0)
    finish(1)
    probe_total.stages(4)
    probe_total.stages(5)
    finish(0)
    probe_total.stages(6)
    probe_total.stages(7)
    probe_total.drain()
    for copy in copies:
        copy.wait_send()

    @pl.when(core == 1)
    def _():
        wait_bytes(side_spectrum, sent.at[17])


def last_kernel(grads, arrived, total, object_gradient, probe_gradient, summed, written):
    copies = []

    def write(source, target):
        copies.append(pltpu.make_async_copy(source, target, written.at[len(copies)]))
        copies[-1].start()

    spots = [(first, second) for first in range(2) for second in range(2)]
    for spot in spots:
        write(total.at[spot], probe_gradient.at[spot])
    for spot in spots:
        summed[spot] = grads[spot] + arrived[spot]
        write(summed.at[spot], object_gradient.at[spot])
    for copy in copies:
        copy.wait()


def on_device(object_field, probe, scan_positions, amplitudes):
    full, plane = (2, 2, WIDTH, WIDTH), (WIDTH, WIDTH)
    vmem = lambda *dims: pltpu.VMEM(dims, f32)
    anywhere = pl.BlockSpec(memory_space=pltpu.HBM)
    table = jnp.asarray(tables())
    operands = (scan_positions.reshape(1, 2), object_field, probe, amplitudes[0, 0, 0], table)
    grads, arrived, total = pl.pallas_call(
        whole_kernel,
        out_shape=[jax.ShapeDtypeStruct(full, f32)] * 3,
        in_specs=[pl.BlockSpec(memory_space=pltpu.SMEM)] + [anywhere] * 4,
        out_specs=[pl.BlockSpec(memory_space=pltpu.VMEM)] * 3,
        scratch_shapes=[
            vmem(*full), vmem(*full), vmem(*plane), pltpu.VMEM(table.shape, bf16), pltpu.SemaphoreType.DMA((4,)),
            vmem(*full), vmem(*full), vmem(*full),
            pltpu.VMEM((8, WIDTH), jnp.int32), pltpu.VMEM((8, WIDTH), jnp.int32),
            vmem(*full), vmem(*full), vmem(*full), vmem(*plane), vmem(*plane), vmem(*plane),
            pltpu.SemaphoreType.DMA((18,)), pltpu.SemaphoreType.DMA((18,)), pltpu.SemaphoreType.REGULAR((3, 2, 5)),
            vmem(*full), vmem(*full), vmem(*full), vmem(*full),
            pltpu.SemaphoreType.DMA((4,)), pltpu.SemaphoreType.DMA((4,)),
            *PROBE_SUM_SCRATCH,
        ],
        compiler_params=pltpu.CompilerParams(collective_id=0, has_side_effects=True, vmem_limit_bytes=40 << 20),
    )(*(pltpu.with_memory_space_constraint(x, pltpu.HBM) for x in operands))
    return tuple(
        pl.pallas_call(
            last_kernel,
            out_shape=[jax.ShapeDtypeStruct(full, f32)] * 2,
            in_specs=[pl.BlockSpec(memory_space=pltpu.VMEM)] * 3,
            out_specs=[anywhere] * 2,
            scratch_shapes=[vmem(*full), pltpu.SemaphoreType.DMA((8,))],
            compiler_params=pltpu.CompilerParams(vmem_limit_bytes=8 << 20),
        )(grads, arrived, total)
    )


def solution(mesh):
    in_specs = (
        P(None, None, "row", "col"),
        P(),
        P("row", "col", None, None),
        P("row", "col", None, None, None),
    )
    out_specs = (P(None, None, "row", "col"), P())
    return jax.shard_map(
        on_device, mesh=mesh, in_specs=in_specs, out_specs=out_specs, check_vma=False
    )
```

```python
import functools
import math

import jax
import jax.numpy as jnp
import ml_dtypes
import numpy as np
from jax import lax
from jax.experimental import pallas as pl
from jax.experimental.pallas import tpu as pltpu
from jax.sharding import PartitionSpec as P

intensity_floor = 0.5
chirp_divisor = 2.0
WIDTH = 256
HALF = 128
ROWS, COLS = 64, 12
f32, bf16 = jnp.float32, jnp.bfloat16


def right_form(matrix):
    return np.block([[matrix.real, matrix.imag], [-matrix.imag, matrix.real]])


def left_form(matrix):
    return np.block([[matrix.real, -matrix.imag], [matrix.imag, matrix.real]])


@functools.lru_cache
def tables():
    indices = np.arange(WIDTH)
    turns = (indices[:, None] * indices[None, :]) % WIDTH
    dft = np.exp(-2j * np.pi * turns / WIDTH) / np.sqrt(WIDTH)
    centered = np.where(indices < HALF, indices, indices - WIDTH).astype(np.float64)
    phase = np.exp(-1j * np.pi * centered**2 / (chirp_divisor * WIDTH))
    kernel = np.conj(dft) @ (phase[:, None] * dft)
    near, far = kernel[:HALF, :HALF], kernel[:HALF, HALF:]
    halves = [(near + far) / 2, (near - far) / 2]
    combs = [dft[:HALF, 0::2], dft[:HALF, 1::2]]
    blocks = np.stack(
        [
            [right_form(m) for m in halves],
            [left_form(m) for m in halves],
            [right_form(m) for m in combs],
            [left_form(m.T) for m in combs],
        ]
    )
    high = blocks.astype(np.float32).astype(ml_dtypes.bfloat16)
    low = (blocks - high.astype(np.float64)).astype(np.float32).astype(ml_dtypes.bfloat16)
    return np.stack([high, low], axis=2)


KERNEL, KERNEL_BACK, DFT, DFT_BACK = (0, 1), (1, 0), (2, 3), (3, 2)


def split(value):
    high = value.astype(bf16)
    return high, (value - high.astype(f32)).astype(bf16)


def times_right(field, table):
    high, low = split(field)
    blocks = jnp.concatenate([table[0], table[0], table[1]], axis=0)
    return jnp.dot(jnp.concatenate([high, low, high], axis=1), blocks, preferred_element_type=f32)


def times_left(table, field):
    high, low = split(field)
    blocks = jnp.concatenate([table[0], table[1], table[0]], axis=1)
    return jnp.dot(blocks, jnp.concatenate([high, high, low], axis=0), preferred_element_type=f32)


def both_sides(combs, table, sides):
    right, left = sides
    turned = [times_right(combs[e], table[right, e]) for e in range(2)]
    out = []
    for e in range(2):
        slabs = []
        for start in range(e * HALF, combs[0].shape[0], WIDTH):
            rows = [turned[k][start : start + HALF] for k in range(2)]
            top = jnp.concatenate([rows[0][:, :HALF], rows[1][:, :HALF]], axis=1)
            bottom = jnp.concatenate([rows[0][:, HALF:], rows[1][:, HALF:]], axis=1)
            slabs.append(jnp.concatenate([top, bottom], axis=0))
        out.append(times_left(table[left, e], jnp.concatenate(slabs, axis=1)))
    return out


def butterfly(plane):
    plane = jnp.concatenate([plane[:HALF] + plane[HALF:], plane[:HALF] - plane[HALF:]], axis=0)
    return plane[:, :HALF] + plane[:, HALF:], plane[:, :HALF] - plane[:, HALF:]


def fold(waves):
    parts = [(butterfly(re), butterfly(im)) for re, im in waves]
    return [
        jnp.concatenate([jnp.concatenate([re[e], im[e]], axis=1) for re, im in parts], axis=0) for e in range(2)
    ]


def comb_fields(fields):
    return [
        jnp.concatenate(
            [jnp.concatenate([part[:, e * HALF : (e + 1) * HALF] for part in pair], axis=1) for pair in fields], axis=0
        )
        for e in range(2)
    ]


def plane_of(out, mode, part):
    lanes = slice(mode * WIDTH, (mode + 1) * WIDTH)
    rows = slice(part * HALF, (part + 1) * HALF)
    return [out[e][rows, lanes] for e in range(2)]


def unfold(out):
    def spread(mode, part):
        even, odd = plane_of(out, mode, part)
        plane = jnp.concatenate([even + odd, even - odd], axis=0)
        even, odd = plane[:, :HALF], plane[:, HALF:]
        return jnp.concatenate([even + odd, even - odd], axis=1)

    return [(spread(mode, 0), spread(mode, 1)) for mode in range(out[0].shape[1] // WIDTH)]


def in_combs(out):
    return [tuple(jnp.concatenate(plane_of(out, mode, part), axis=0) for part in range(2)) for mode in range(2)]


def times(a, b):
    return a[0] * b[0] - a[1] * b[1], a[0] * b[1] + a[1] * b[0]


def times_conj(a, b):
    return a[0] * b[0] + a[1] * b[1], a[1] * b[0] - a[0] * b[1]


def iota(axis):
    return lax.broadcasted_iota(jnp.int32, (WIDTH, WIDTH), axis)


def one_hot(condition):
    return jnp.where(condition, 1.0, 0.0).astype(bf16)


def permute(left, planes, right):
    count = len(planes)
    high, low = split(jnp.concatenate(planes, axis=1))
    moved = jnp.dot(left, high, preferred_element_type=f32) + jnp.dot(left, low, preferred_element_type=f32)
    rows = jnp.concatenate([moved[:, k * WIDTH : (k + 1) * WIDTH] for k in range(count)], axis=0)
    high, low = split(rows)
    moved = jnp.dot(high, right, preferred_element_type=f32) + jnp.dot(low, right, preferred_element_type=f32)
    return [moved[k * WIDTH : (k + 1) * WIDTH] for k in range(count)]


MESH_ID = pl.DeviceIdType.MESH


def place():
    row = lax.axis_index("row")
    return row // 16, (row // 2) % 8, lax.axis_index("col"), row % 2


def device(x, y, z, core):
    return ((x * 8 + y) * 2 + core, z)


def start_copy(source, target, sent, landed, to):
    copy = pltpu.make_async_remote_copy(
        src_ref=source, dst_ref=target, send_sem=sent, recv_sem=landed, device_id=to, device_id_type=MESH_ID
    )
    copy.start()
    return copy


def wait_bytes(ref, semaphore):
    pltpu.make_async_copy(ref, ref, semaphore).wait()


class ProbeSum:
    GRAIN = (4, 4, 4, 4, 4, 4, 4, 4)

    def __init__(self, parts, total, from_core, near, from_x, mid, from_y, from_z, sent, landed):
        self.parts, self.total, self.from_core, self.near = parts, total, from_core, near
        self.from_x, self.mid, self.from_y, self.from_z = from_x, mid, from_y, from_z
        self.sent, self.landed = sent, landed
        self.x, self.y, self.z, self.core = place()
        self.arrived = set()

    def x_peers(self):
        return [lax.rem(self.x + d, 4) for d in (2, 1, 3)]

    def y_peers(self):
        return [lax.rem(self.y + d, 8) for d in (4, 3, 5, 2, 6, 1, 7)]

    def z_peers(self):
        return [lax.rem(self.z + d, 12) for d in (6, 5, 7, 4, 8, 3, 9, 2, 10, 1, 11)]

    def cut(self, step, unit):
        grain = self.GRAIN[step]
        if grain == 1:
            return slice(0, 2), slice(0, 256)
        if grain == 2:
            return slice(unit, unit + 1), slice(0, 256)
        return slice(unit // 2, unit // 2 + 1), slice(128 * (unit % 2), 128 * (unit % 2) + 128)

    def volume(self, step, unit):
        modes, lanes = self.cut(step, unit)
        modes, lanes = pl.ds(modes.start, modes.stop - modes.start), pl.ds(lanes.start, lanes.stop - lanes.start)
        if step == 0:
            return self.from_core.at[modes, :, lanes]
        if step == 1:
            return self.from_x.at[:, modes, :, lanes]
        if step == 2:
            return self.from_y.at[:, modes, :, lanes]
        if step == 3:
            return self.from_z.at[pl.ds(0, 11), modes, :, lanes]
        rows = {4: 56, 5: 192, 6: 256}[step]
        return self.total.at[modes, self.core, pl.ds(0, rows), lanes]

    def await_step(self, step, modes, lanes):
        for unit in range(self.GRAIN[step]):
            m, l = self.cut(step, unit)
            apart = m.stop <= modes.start or modes.stop <= m.start or l.stop <= lanes.start or lanes.stop <= l.start
            if not apart and (step, unit) not in self.arrived:
                self.arrived.add((step, unit))
                wait_bytes(self.volume(step, unit), self.landed.at[step, unit])

    def stage(self, step, unit):
        x, y, z, core = self.x, self.y, self.z, self.core
        modes, lanes = self.cut(step, unit)
        if step > 0:
            self.await_step(step - 1, modes, lanes)
        if step == 7:
            return
        m, l = pl.ds(modes.start, modes.stop - modes.start), pl.ds(lanes.start, lanes.stop - lanes.start)
        sent, landed = self.sent.at[step, unit], self.landed.at[step, unit]
        other = device(x, y, z, 1 - core)
        mine = pl.ds(pl.multiple_of(64 * x + 8 * y, 8), 8)
        block = pl.ds(pl.multiple_of(64 * x, 64), 64)
        if step == 0:
            start_copy(self.parts.at[m, 1 - core, :, l], self.from_core.at[m, :, l], sent, landed, other)
        elif step == 1:
            self.near[m, :, l] = self.parts[m, core, :, l] + self.from_core[m, :, l]
            for d, px in enumerate(self.x_peers()):
                rows = pl.ds(pl.multiple_of(64 * px, 64), 64)
                start_copy(self.near.at[m, rows, l], self.from_x.at[d, m, :, l], sent, landed, device(px, y, z, core))
        elif step == 2:
            self.mid[m, :, l] = (self.near[m, block, l] + self.from_x[0, m, :, l]) + (
                self.from_x[1, m, :, l] + self.from_x[2, m, :, l]
            )
            for d, py in enumerate(self.y_peers()):
                rows = pl.ds(pl.multiple_of(8 * py, 8), 8)
                start_copy(self.mid.at[m, rows, l], self.from_y.at[d, m, :, l], sent, landed, device(x, py, z, core))
        elif step == 3:
            piece = self.mid[m, pl.ds(pl.multiple_of(8 * y, 8), 8), l]
            for d in range(7):
                piece = piece + self.from_y[d, m, :, l]
            self.from_z[z, m, :, l] = piece
            spot = self.from_z.at[z, m, :, l]
            for pz in self.z_peers():
                start_copy(spot, spot, sent, landed, device(x, y, pz, core))
        elif step == 4:
            piece = self.from_z[0, m, :, l]
            for d in range(1, 12):
                piece = piece + self.from_z[d, m, :, l]
            self.total[m, core, mine, l] = piece * (1.0 / math.sqrt(ROWS * COLS))
            spot = self.total.at[m, core, mine, l]
            for py in self.y_peers():
                start_copy(spot, spot, sent, landed, device(x, py, z, core))
        elif step == 5:
            spot = self.total.at[m, core, block, l]
            for px in self.x_peers():
                start_copy(spot, spot, sent, landed, device(px, y, z, core))
        elif step == 6:
            spot = self.total.at[m, core, :, l]
            start_copy(spot, spot, sent, landed, other)

    def stages(self, step):
        for unit in range(self.GRAIN[step]):
            self.stage(step, unit)

    def drain(self):
        for step in range(7):
            for unit in range(self.GRAIN[step]):
                wait_bytes(self.volume(step, unit), self.sent.at[step, unit])

    REACH = (2, 4, 6)

    def beside(self, axis, by):
        x, y, z, core = self.x, self.y, self.z, self.core
        if axis == 0:
            return device(lax.rem(x + 4 + by, 4), y, z, core)
        if axis == 1:
            return device(x, lax.rem(y + 8 + by, 8), z, core)
        return device(x, y, lax.rem(z + 12 + by, 12), core)

    def greet(self, barrier):
        peers = [device(self.x, self.y, self.z, 1 - self.core)]
        peers += [self.beside(axis, by) for axis in range(3) for by in (1, -1)]
        for peer in peers:
            pl.semaphore_signal(barrier, inc=1, device_id=peer, device_id_type=MESH_ID)
        return len(peers)

    def pass_word(self, words, distance):
        for axis, reach in enumerate(self.REACH):
            for way, by in enumerate((1, -1)):
                if 2 < distance <= reach + 1:
                    pl.semaphore_wait(words.at[axis, way, distance - 3], 1)
                if distance <= reach:
                    word = words.at[axis, way, distance - 2]
                    pl.semaphore_signal(word, inc=1, device_id=self.beside(axis, by), device_id_type=MESH_ID)


PROBE_SUM_SCRATCH = [
    pltpu.VMEM((2, 256, 256), jnp.float32),
    pltpu.VMEM((2, 256, 256), jnp.float32),
    pltpu.VMEM((3, 2, 64, 256), jnp.float32),
    pltpu.VMEM((2, 64, 256), jnp.float32),
    pltpu.VMEM((7, 2, 8, 256), jnp.float32),
    pltpu.VMEM((12, 2, 8, 256), jnp.float32),
    pltpu.SemaphoreType.DMA((7, 4)),
    pltpu.SemaphoreType.DMA((7, 4)),
]


def whole_kernel(
    position, tile_in, probe_in, amplitude_in, table_in,
    grads, down_in, total,
    tile, probe, amplitude, table, loads,
    patch, moved_probe, wave, corner, left_corner, below, merged, side, own_spectrum, side_spectrum, spectrum, sent, landed, words,
    parts, side_out, side_in, down_out, back_sent, back_landed, *scratch,
):
    def load(source, target, index):
        copy = pltpu.make_async_copy(source, target, loads.at[index])
        copy.start()
        return copy

    row, z = lax.axis_index("row"), lax.axis_index("col")
    core = lax.rem(row, 2)
    up, down = (lax.rem(row + ROWS - 1, ROWS), z), (lax.rem(row + 1, ROWS), z)
    right = (row, lax.rem(z + 1, COLS))
    onward = (row, lax.rem(z + COLS - 1 + 2 * core, COLS))
    back = (row, lax.rem(z + 1 + (COLS - 2) * core, COLS))
    probe_total = ProbeSum(parts, total, *scratch)

    loading = [
        load(source, target, index)
        for index, (source, target) in enumerate(
            [(amplitude_in, amplitude), (tile_in, tile), (probe_in, probe), (table_in, table)]
        )
    ]
    barrier = pltpu.get_barrier_semaphore()
    count = probe_total.greet(barrier)
    for peer in (up, down):
        pl.semaphore_signal(barrier, inc=1, device_id=peer, device_id_type=MESH_ID)

    rows, lanes = iota(0), iota(1)
    first_row = lax.broadcasted_iota(jnp.int32, (8, WIDTH), 0) == 0
    corner[...] = jnp.where(first_row, position[0, 0] - row * WIDTH, position[0, 1] - z * WIDTH)
    to_combs = one_hot(lanes == 2 * lax.rem(rows, HALF) + rows // HALF)
    from_combs = one_hot(rows == 2 * lax.rem(lanes, HALF) + lanes // HALF)
    loading[0].wait()
    own_spectrum[...] = permute(to_combs, [amplitude[...]], from_combs)[0]
    for copy in loading[1:]:
        copy.wait()
    pl.semaphore_wait(barrier, count + 2)

    def chunk(index):
        layer, part, half = index // 4, (index // 2) % 2, index % 2
        return layer, part, pl.ds(half * HALF, HALF)

    copies = [start_copy(corner, left_corner, sent.at[16], landed.at[16], right)]
    for index in range(8):
        spot = chunk(index)
        copies.append(start_copy(tile.at[spot], below.at[spot], sent.at[index], landed.at[index], up))

    @pl.when(core == 1)
    def _():
        start_copy(own_spectrum, side_spectrum, sent.at[17], landed.at[17], right)

    probe_total.pass_word(words, 2)
    wait_bytes(left_corner, landed.at[16])
    own, other = corner[...], left_corner[...]
    working = own + core * (other - own)
    handing = other + core * (own - other)
    row_start, col_start, hand_start = working[0:1, :], working[1:2, :], handing[0:1, :]
    own_columns = jnp.where(lanes >= col_start, 1, 0) != core

    for index in range(8):
        layer, part, span = chunk(index)
        wait_bytes(below.at[layer, part, span], landed.at[index])
        mine, under = tile[layer, part, span, :], below[layer, part, span, :]
        merged[layer, part, span, :] = jnp.where(rows[span.start : span.start + HALF] >= hand_start, mine, under)
        spot = merged.at[layer, part, span]
        copies.append(start_copy(spot, side.at[layer, part, span], sent.at[8 + index], landed.at[8 + index], onward))
        patch[layer, part, span, :] = jnp.where(rows[span.start : span.start + HALF] >= row_start, mine, under)
        if index % 2:
            probe_total.pass_word(words, 3 + index // 2)
        if index == 7:
            shift_rows = one_hot(jnp.bitwise_and(rows - lanes - row_start, WIDTH - 1) == 0)
            shift_cols = one_hot(jnp.bitwise_and(lanes - rows - col_start, WIDTH - 1) == 0)
            planes = [probe[mode, part] for mode in range(2) for part in range(2)]
            for k, plane in enumerate(permute(shift_rows, planes, shift_cols)):
                moved_probe[k // 2, k % 2] = plane

    def patch_of(layer):
        for index in range(4):
            wait_bytes(side.at[chunk(4 * layer + index)], landed.at[8 + 4 * layer + index])
        pair = tuple(jnp.where(own_columns, patch[layer, part], side[layer, part]) for part in range(2))
        patch[layer, 0], patch[layer, 1] = pair
        return pair

    first = patch_of(0)
    waves = [times((moved_probe[mode, 0], moved_probe[mode, 1]), first) for mode in range(2)]
    for mode, pair in enumerate(unfold(both_sides(fold(waves), table, KERNEL))):
        wave[mode, 0], wave[mode, 1] = pair
    probe_total.pass_word(words, 7)
    second = patch_of(1)

    @pl.when(core == 0)
    def _():
        spectrum[...] = own_spectrum[...]

    @pl.when(core == 1)
    def _():
        wait_bytes(side_spectrum, landed.at[17])
        spectrum[...] = side_spectrum[...]

    waves = [(wave[mode, 0], wave[mode, 1]) for mode in range(2)]
    far = in_combs(both_sides(fold([times(pair, second) for pair in waves]), table, DFT))
    intensity = far[0][0] * far[0][0] + far[0][1] * far[0][1] + (far[1][0] * far[1][0] + far[1][1] * far[1][1])
    weight = 2.0 - 2.0 * spectrum[...] * lax.rsqrt(intensity + intensity_floor)
    far = [(weight * re, weight * im) for re, im in far]
    slope = unfold(both_sides(comb_fields(far), table, DFT_BACK))

    def send_side(layer, terms):
        for part in range(2):
            grads[layer, part] = terms[0][part] + terms[1][part]
            side_out[layer, part] = jnp.where(own_columns, 0.0, grads[layer, part])
        copies.append(
            start_copy(side_out.at[layer], side_in.at[layer], back_sent.at[layer], back_landed.at[layer], back)
        )

    def send_down(layer):
        wait_bytes(side_in.at[layer], back_landed.at[layer])
        for part in range(2):
            mine = jnp.where(own_columns, grads[layer, part], 0.0)
            other = side_in[layer, part]
            down_out[layer, part] = jnp.where(rows < row_start, mine, 0.0) + jnp.where(rows < hand_start, other, 0.0)
            grads[layer, part] = jnp.where(rows < row_start, 0.0, mine) + jnp.where(rows < hand_start, 0.0, other)
        copies.append(
            start_copy(
                down_out.at[layer], down_in.at[layer], back_sent.at[2 + layer], back_landed.at[2 + layer], down
            )
        )

    def finish(layer):
        wait_bytes(down_in.at[layer], back_landed.at[2 + layer])

    send_side(1, [times_conj(slope[mode], waves[mode]) for mode in range(2)])
    shift_rows = one_hot(jnp.bitwise_and(lanes - rows - row_start, WIDTH - 1) == 0)
    shift_cols = one_hot(jnp.bitwise_and(rows - lanes - col_start, WIDTH - 1) == 0)
    first, second = (patch[0, 0], patch[0, 1]), (patch[1, 0], patch[1, 1])
    terms = []
    for mode in range(2):
        bent = unfold(both_sides(fold([times_conj(slope[mode], second)]), table, KERNEL_BACK))[0]
        if mode == 1:
            probe_total.stage(1, 0)
            probe_total.stage(1, 1)
        for part, plane in enumerate(permute(shift_rows, list(times_conj(bent, first)), shift_cols)):
            parts[mode, part] = plane
        probe_total.stage(0, 2 * mode)
        probe_total.stage(0, 2 * mode + 1)
        terms.append(times_conj(bent, (moved_probe[mode, 0], moved_probe[mode, 1])))
    send_side(0, terms)
    probe_total.stage(1, 2)
    probe_total.stage(1, 3)
    probe_total.stages(2)
    probe_total.stages(3)
    send_down(1)
    probe_total.stages(4)
    probe_total.stages(5)
    send_down(0)
    probe_total.stages(6)
    finish(1)
    probe_total.stages(7)
    finish(0)
    probe_total.drain()
    for copy in copies:
        copy.wait_send()

    @pl.when(core == 1)
    def _():
        wait_bytes(side_spectrum, sent.at[17])


def last_kernel(grads, arrived, total, object_gradient, probe_gradient, summed, written):
    copies = []

    def write(source, target):
        copies.append(pltpu.make_async_copy(source, target, written.at[len(copies)]))
        copies[-1].start()

    spots = [(first, second) for first in range(2) for second in range(2)]
    for spot in spots:
        write(total.at[spot], probe_gradient.at[spot])
    for spot in spots:
        summed[spot] = grads[spot] + arrived[spot]
        write(summed.at[spot], object_gradient.at[spot])
    for copy in copies:
        copy.wait()


def on_device(object_field, probe, scan_positions, amplitudes):
    full, plane = (2, 2, WIDTH, WIDTH), (WIDTH, WIDTH)
    vmem = lambda *dims: pltpu.VMEM(dims, f32)
    anywhere = pl.BlockSpec(memory_space=pltpu.HBM)
    table = jnp.asarray(tables())
    operands = (scan_positions.reshape(1, 2), object_field, probe, amplitudes[0, 0, 0], table)
    grads, arrived, total = pl.pallas_call(
        whole_kernel,
        out_shape=[jax.ShapeDtypeStruct(full, f32)] * 3,
        in_specs=[pl.BlockSpec(memory_space=pltpu.SMEM)] + [anywhere] * 4,
        out_specs=[pl.BlockSpec(memory_space=pltpu.VMEM)] * 3,
        scratch_shapes=[
            vmem(*full), vmem(*full), vmem(*plane), pltpu.VMEM(table.shape, bf16), pltpu.SemaphoreType.DMA((4,)),
            vmem(*full), vmem(*full), vmem(*full),
            pltpu.VMEM((8, WIDTH), jnp.int32), pltpu.VMEM((8, WIDTH), jnp.int32),
            vmem(*full), vmem(*full), vmem(*full), vmem(*plane), vmem(*plane), vmem(*plane),
            pltpu.SemaphoreType.DMA((18,)), pltpu.SemaphoreType.DMA((18,)), pltpu.SemaphoreType.REGULAR((3, 2, 5)),
            vmem(*full), vmem(*full), vmem(*full), vmem(*full),
            pltpu.SemaphoreType.DMA((4,)), pltpu.SemaphoreType.DMA((4,)),
            *PROBE_SUM_SCRATCH,
        ],
        compiler_params=pltpu.CompilerParams(collective_id=0, has_side_effects=True, vmem_limit_bytes=40 << 20),
    )(*(pltpu.with_memory_space_constraint(x, pltpu.HBM) for x in operands))
    return tuple(
        pl.pallas_call(
            last_kernel,
            out_shape=[jax.ShapeDtypeStruct(full, f32)] * 2,
            in_specs=[pl.BlockSpec(memory_space=pltpu.VMEM)] * 3,
            out_specs=[anywhere] * 2,
            scratch_shapes=[vmem(*full), pltpu.SemaphoreType.DMA((8,))],
            compiler_params=pltpu.CompilerParams(vmem_limit_bytes=8 << 20),
        )(grads, arrived, total)
    )


def solution(mesh):
    in_specs = (
        P(None, None, "row", "col"),
        P(),
        P("row", "col", None, None),
        P("row", "col", None, None, None),
    )
    out_specs = (P(None, None, "row", "col"), P())
    return jax.shard_map(
        on_device, mesh=mesh, in_specs=in_specs, out_specs=out_specs, check_vma=False
    )
```
